32 devices in a mesh: rep: 4 (over y, core), shard: 8 (over z, x).
Axes of the slice: x: 2, y: 2, z: 4, core: 2. Of those that a mesh axis runs over, the one named last changes fastest.
Arguments:
- grad_part: bfloat16 [4, 4096, 512], P('rep', 'shard'), may hold values from -10.5 to 10.5
- seg_slot: int32 [8, 512], replicated, may hold values from 0 to 4095, as said below
- owner: int32 [8], replicated, may hold values from 0 to 7, as said below
- left_code: bfloat16 [16, 512, 512], P('shard'), may hold values from -127 to 127, as said below
- left_scale: float32 [16, 512], P('shard'), may hold values from 0.0023622 to 0.023622
- right_code: bfloat16 [16, 512, 512], P('shard'), may hold values from -127 to 127, as said below
- right_scale: float32 [16, 512], P('shard'), may hold values from 0.0023622 to 0.023622
Outputs:
- update: bfloat16 [4096, 512], P('shard')
The draws below stay inside these ranges and needn't reach their ends.
Inputs may be any that keep to these rules, and one draw needn't show every extreme that they name: `seg_slot`: every flat segment index appears once; row i of block b lies in shard (i + c) mod 8, where c, drawn for each block, is the shard of its row 0, and shard k holds the segment indices k * 512 to (k + 1) * 512 - 1. `owner`: no shard index owns more than 2 blocks, and one owns exactly 2. `left_code`: whole numbers; each row's largest code has magnitude 127. `right_code`: whole numbers; each column's largest code has magnitude 127.
All inputs are finite; a program needn't handle non-finite values.
Results may differ from the reference program's by a relative error of at most 0.025.
Values may be sent and summed in bfloat16 or wider, within the bound.
A program may use at most 64 MiB of HBM per device.

```python
import math
import jax
import jax.numpy as jnp
from jax import lax

B = 512
NBLK = 8
SLOTS = 2
ROWS_SHARD = 64
SEGS = 4096
SEGS_DEV = 512
SLOT_ALL = 16
N_REP = 4
N_SHARD = 8


def root_code(key, spread):
    offdiag = jax.random.uniform(key, (SLOT_ALL, B, B), jnp.float32, -spread, spread)
    mirror = 0.5 * (offdiag + jnp.swapaxes(offdiag, 1, 2))
    levels = jnp.floor(mirror * 127.0 + 0.5)
    identity = jnp.eye(B, dtype=jnp.float32)
    return (127.0 * identity + levels * (1.0 - identity)).astype(jnp.bfloat16)


def draw_left_code(key, part):
    key = jax.random.fold_in(key, 11)
    return root_code(key, 0.1)


def draw_right_code(key, part):
    key = jax.random.fold_in(key, 13)
    return root_code(key, 0.1)


def draw_grad_part(key, part):
    key = jax.random.fold_in(key, 5)
    key_rows, key_cols, key_private = jax.random.split(key, 3)
    spread_log = 1.15
    values = jnp.clip(jax.random.normal(key_private, (N_REP, SEGS, B), jnp.float32), -4.0, 4.0)
    row_scale = jnp.exp(jax.random.uniform(key_rows, (1, SEGS, 1), jnp.float32, -spread_log, spread_log))
    col_scale = jnp.exp(jax.random.uniform(key_cols, (1, 1, B), jnp.float32, -spread_log, spread_log))
    return (0.25 * values * row_scale * col_scale).astype(jnp.bfloat16)


def shard_order(subkey):
    return jax.random.permutation(subkey, SEGS_DEV)


def draw_seg_slot(key, part):
    key = jax.random.fold_in(key, 7)
    key_shift, key_order = jax.random.split(key)
    first_shard = jax.random.randint(key_shift, (NBLK, 1), 0, N_SHARD)
    row_index = jnp.arange(B, dtype=jnp.int32)[None, :]
    holder = (row_index % N_SHARD + first_shard) % N_SHARD
    canonical = jnp.arange(NBLK, dtype=jnp.int32)[:, None] * ROWS_SHARD + row_index // N_SHARD
    orders = jax.vmap(shard_order)(jax.random.split(key_order, N_SHARD)).astype(jnp.int32)
    return (holder * SEGS_DEV + orders[holder, canonical]).astype(jnp.int32)


def move_front(order_list, value, place):
    found = jnp.argmax((order_list == value).astype(jnp.int32)).astype(jnp.int32)
    current = order_list[place]
    return order_list.at[found].set(current).at[place].set(value)


def draw_owner(key, part):
    key = jax.random.fold_in(key, 3)
    key_busy, key_fill, key_place = jax.random.split(key, 3)
    busiest = jax.random.randint(key_busy, (), 0, N_SHARD).astype(jnp.int32)
    order_list = jax.random.permutation(key_fill, (N_SHARD - 1) * SLOTS).astype(jnp.int32)
    order_list = move_front(order_list, jnp.int32(0), 0)
    order_list = move_front(order_list, jnp.int32((N_SHARD - 2) * SLOTS), 1)
    others = order_list[:NBLK - SLOTS] // SLOTS
    others = others + (others >= busiest).astype(jnp.int32)
    listed = jnp.concatenate([jnp.full((SLOTS,), busiest, jnp.int32), others])
    return jax.random.permutation(key_place, listed).astype(jnp.int32)


def level_of(key, shape, pieces, smallest, top_value):
    factor_of = 1.0
    for position, shards_of in pieces:
        heights = jax.random.uniform(jax.random.fold_in(jax.random.fold_in(key, 6), position), (shards_of,), jnp.float32, smallest / len(pieces), top_value / len(pieces))
        factor_of = factor_of * jnp.repeat(jnp.exp(heights), shape[position] // shards_of).reshape((-1,) + (1,) * (len(shape) - 1 - position))
    return factor_of


def setup_inputs(seed: int = 0) -> dict:
    splits = jax.random.split(jax.random.key(seed), 8)
    grad_part = draw_grad_part(jax.random.fold_in(splits[7], 71), 0)
    seg_slot = draw_seg_slot(jax.random.fold_in(splits[7], 71), 0)
    owner = draw_owner(jax.random.fold_in(splits[7], 71), 0)
    left_code = draw_left_code(jax.random.fold_in(splits[7], 71), 0)
    left_scale = jnp.clip(jnp.exp(math.log(0.023622) - 2.3025851 * jax.random.uniform(splits[4], (SLOT_ALL, B), jnp.float32) ** level_of(splits[4], (SLOT_ALL, B), ((0, 8),), -0.2, 0.2)), 0.0023622, 0.023622)
    right_code = draw_right_code(jax.random.fold_in(splits[7], 71), 0)
    right_scale = jnp.clip(jnp.exp(math.log(0.023622) - 2.3025851 * jax.random.uniform(splits[6], (SLOT_ALL, B), jnp.float32) ** level_of(splits[6], (SLOT_ALL, B), ((0, 8),), -0.2, 0.2)), 0.0023622, 0.023622)
    return {"grad_part": grad_part, "seg_slot": seg_slot, "owner": owner, "left_code": left_code, "left_scale": left_scale, "right_code": right_code, "right_scale": right_scale}


EPSILON = 1e-06

def slot_numbers(owner):
    block_ids = jnp.arange(owner.shape[0], dtype=jnp.int32)
    same_owner = owner[None, :] == owner[:, None]
    earlier = block_ids[None, :] < block_ids[:, None]
    slot_rank = lax.optimization_barrier(jnp.sum((same_owner & earlier).astype(jnp.int32), axis=1))
    return (owner * SLOTS + slot_rank).astype(jnp.int32)

def reference(grad_part, seg_slot, owner, left_code, left_scale, right_code, right_scale):
    grad = lax.optimization_barrier(jnp.sum(grad_part.astype(jnp.float32), axis=0)).astype(jnp.bfloat16)
    slot_index = slot_numbers(owner)

    def one_block(inputs):
        row_ids, slot_id = inputs
        block_grad = grad[row_ids]
        middle = jnp.dot(block_grad, right_code[slot_id], preferred_element_type=jnp.float32)
        middle = (middle * right_scale[slot_id][None, :]).astype(jnp.bfloat16)
        precond = jnp.dot(left_code[slot_id], middle, preferred_element_type=jnp.float32)
        precond = precond * left_scale[slot_id][:, None]
        grad_wide = block_grad.astype(jnp.float32)
        graft_ratio = jnp.sqrt((jnp.mean(grad_wide * grad_wide) + EPSILON) / (jnp.mean(precond * precond) + EPSILON))
        return (precond * graft_ratio).astype(jnp.bfloat16)
    update_block = lax.map(one_block, (seg_slot, slot_index))
    update = jnp.zeros((SEGS, B), jnp.bfloat16)
    return update.at[seg_slot.reshape(-1)].set(update_block.reshape(-1, B))
```

```python
import functools

import jax
import jax.numpy as jnp
from jax import lax
from jax.experimental import pallas as pl
from jax.experimental.pallas import tpu as pltpu
from jax.sharding import PartitionSpec as P

EPSILON = 1e-06
MESH = pl.DeviceIdType.MESH
F32 = jnp.float32
BF16 = jnp.bfloat16
Y_OUT, Z_OUT, C_OUT, Z_BACK, Y_BACK, C_BACK, C_BACK_FAR, PAIR = range(8)


def log2(value):
    assert value & (value - 1) == 0
    return value.bit_length() - 1


def iota(shape, dim):
    return lax.broadcasted_iota(jnp.int32, shape, dim)


def one_hot(mask):
    return jnp.where(mask, 1.0, 0.0).astype(BF16)


def dot(a, b, contract=((1,), (0,))):
    return lax.dot_general(a, b, (contract, ((), ())), preferred_element_type=F32)


def partner(me, k, shards):
    out = 0
    for j in range(log2(shards)):
        bit = lax.rem(lax.div(me, 1 << j), 2)
        out = out + (1 - bit if (k >> j) & 1 else bit) * (1 << j)
    return out


def far_first(shards):
    order = []
    width = shards // 2
    while width:
        order += range(width, 2 * width)
        width //= 2
    return order


def kernel(
    shards, seg_ref, own_col_ref, own_row_ref, lscale_ref, rscale_ref, grad_hbm, left_hbm, right_hbm,
    out_hbm,
    p_own, p_got, wt, f, y_got, g, a, left_v, right_v, lperm, mid, u, ud, o, local_sem, send_sem, recv_sem,
):
    rep, me = lax.axis_index("rep"), lax.axis_index("shard")
    y, c = lax.rem(lax.div(rep, 2), 2), lax.rem(rep, 2)
    y_rep, c_rep = rep + 2 - 4 * y, rep + 1 - 2 * c
    blocks, order_b = seg_ref.shape
    rows = order_b // shards
    seg_local, half = p_own.shape
    flat = shards * rows
    order = far_first(shards)
    peers = {k: partner(me, k, shards) for k in order}
    here = pl.ds(pl.multiple_of(c * half, half), half)
    there = pl.ds(pl.multiple_of((1 - c) * half, half), half)

    loads = [
        pltpu.make_async_copy(grad_hbm.at[0, :, here], p_own, local_sem.at[0]),
        pltpu.make_async_copy(left_hbm.at[y], left_v, local_sem.at[1]),
    ]
    for i, r in enumerate((here, there)):
        for j, w in enumerate((here, there)):
            loads.append(pltpu.make_async_copy(
                right_hbm.at[y, r, w], right_v.at[i, :, pl.ds(j * half, half)], local_sem.at[2 + 2 * i + j]))
    for load in loads:
        load.start()

    def send(kind, k, src, dst, rep_to, shard_to):
        return pltpu.make_async_remote_copy(
            src_ref=src, dst_ref=dst, send_sem=send_sem.at[kind, k], recv_sem=recv_sem.at[kind, k],
            device_id={"rep": rep_to, "shard": shard_to}, device_id_type=MESH)

    barrier = pltpu.get_barrier_semaphore()
    pl.semaphore_signal(barrier, inc=1, device_id={"rep": c_rep, "shard": me}, device_id_type=MESH)
    pl.semaphore_signal(barrier, inc=1, device_id={"rep": y_rep, "shard": me}, device_id_type=MESH)
    for k in order:
        pl.semaphore_signal(barrier, inc=1, device_id={"rep": rep, "shard": peers[k]}, device_id_type=MESH)
    pl.semaphore_wait(barrier, 2 + len(order))

    pair = send(PAIR, 0, grad_hbm.at[0, :, there], p_got, c_rep, me)
    pair.start()

    seg = seg_ref[...]
    local = seg - me * seg_local
    local = jnp.where((local >= 0) & (local < seg_local), local, 0)
    digits = jnp.concatenate([local >> 4, local & 15], axis=0).astype(F32).astype(BF16)
    spread = one_hot((iota((order_b, flat), 0) >> log2(shards)) == (iota((order_b, flat), 1) & (rows - 1)))
    found = dot(digits, spread)
    place_of = found[:blocks] * 16.0 + found[blocks:] + 1.0
    own_col, own_row = own_col_ref[...], own_row_ref[...]
    earlier = iota((blocks, blocks), 1) < iota((blocks, blocks), 0)
    rank = jnp.sum(jnp.where((own_col == own_row) & earlier, 1.0, 0.0), axis=1, keepdims=True)
    key = own_col.astype(F32) * 2.0 + rank
    peer_row = (iota((1, flat), 1) >> log2(rows)) ^ me
    seg_id = iota((seg_local, flat), 0).astype(F32)
    for plane in range(2):
        wanted = (peer_row * 2 + lax.rem(y + plane, 2)).astype(F32)
        place = jnp.sum(jnp.where(key == wanted, place_of, 0.0), axis=0, keepdims=True) - 1.0
        wt[plane] = one_hot(seg_id == place)

    loads[0].wait()
    pair.wait_recv()
    q = (p_own[...].astype(F32) + p_got[...].astype(F32)).astype(BF16)
    f[1] = dot(wt[1], q, ((0,), (0,))).astype(BF16).reshape(shards, rows, half)
    y_out = {k: send(Y_OUT, k, f.at[1, k], y_got.at[k], y_rep, me) for k in order + [0]}
    for k in order + [0]:
        y_out[k].start()
    f[0] = dot(wt[0], q, ((0,), (0,))).astype(BF16).reshape(shards, rows, half)
    z_out = {k: send(Z_OUT, k, g.at[k], a.at[0, k], rep, peers[k]) for k in order}
    c_out = {k: send(C_OUT, k, a.at[0, k], a.at[1, k], c_rep, me) for k in order + [0]}
    for k in order + [0]:
        y_out[k].wait_recv()
        total = (f[0, k].astype(F32) + y_got[k].astype(F32)).astype(BF16)
        if k:
            g[k] = total
            z_out[k].start()
        else:
            a[0, 0] = total
            c_out[0].start()

    mine = key == (me * 2 + y).astype(F32)
    first = (seg[:, 0:1] >> log2(seg_local)).astype(F32)
    shift = jnp.sum(jnp.where(mine, first, 0.0), axis=0, keepdims=True).astype(jnp.int32)
    line = iota((flat, 1), 0)
    target = (line & (rows - 1)) * shards + ((((line >> log2(rows)) ^ me) - shift) & (shards - 1))
    chosen = iota((flat, order_b), 1) == target
    lscale = jnp.where(y == 0, lscale_ref[0:1, :], lscale_ref[1:2, :])
    lscale = jnp.sum(jnp.where(chosen, lscale, 0.0), axis=1, keepdims=True)
    rscale = jnp.where(y == 0, rscale_ref[0:1, :], rscale_ref[1:2, :])
    rscale = jnp.where(c == 0, rscale, jnp.concatenate([rscale[:, half:], rscale[:, :half]], axis=1))
    turn = one_hot(chosen)
    for load in loads[1:]:
        load.wait()
    lperm[...] = dot(dot(turn, left_v[...]).astype(BF16), turn, ((1,), (1,))).astype(BF16)

    for k in order:
        z_out[k].wait_recv()
        c_out[k].start()
    grad_power = jnp.zeros((1, 1), F32)
    near = shards // 2
    c_out[0].wait_recv()
    for low, high in ((near, shards), (0, near)):
        for k in range(max(low, 1), high):
            c_out[k].wait_recv()
        span = (high - low) * rows
        mine_half = a[0, low:high].reshape(span, half)
        other_half = a[1, low:high].reshape(span, half)
        part = dot(mine_half, right_v[0]) + dot(other_half, right_v[1])
        mid[low * rows:high * rows] = (part * rscale).astype(BF16)
        wide, wide_other = mine_half.astype(F32), other_half.astype(F32)
        grad_power += jnp.sum(wide * wide + wide_other * wide_other, keepdims=True)

    precond = dot(lperm[...], mid[...]) * lscale
    update_power = jnp.sum(precond * precond, keepdims=True)
    scale = 1.0 / (order_b * 2 * half)
    ratio = jnp.sqrt((grad_power * scale + EPSILON) / (update_power * scale + EPSILON))
    u[...] = (precond[:, :half] * ratio).astype(BF16).reshape(shards, rows, half)

    z_back = {k: send(Z_BACK, k, u.at[k], ud.at[0, 0, k], rep, peers[k]) for k in order}
    y_back = {k: send(Y_BACK, k, ud.at[0, 0, k], ud.at[1, 0, k], y_rep, me) for k in order + [0]}
    c_back = {k: send(C_BACK, k, ud.at[0, 0, k], ud.at[0, 1, k], c_rep, me) for k in order + [0]}
    c_far = {k: send(C_BACK_FAR, k, ud.at[1, 0, k], ud.at[1, 1, k], c_rep, me) for k in order + [0]}
    for k in order:
        z_back[k].start()
    ud[0, 0, 0] = u[0]
    arrivals = [0] + order
    for n in range(shards + 2):
        if n < shards:
            k = arrivals[n]
            if k:
                z_back[k].wait_recv()
            y_back[k].start()
            c_back[k].start()
        if n >= 2:
            k = arrivals[n - 2]
            y_back[k].wait_recv()
            c_far[k].start()

    def placed(side):
        return (dot(wt[0], ud[0, side].reshape(flat, half)) + dot(wt[1], ud[1, side].reshape(flat, half))).astype(BF16)

    o[0] = placed(0)
    write_own = pltpu.make_async_copy(o.at[0], out_hbm.at[:, here], local_sem.at[0])
    write_own.start()
    for k in arrivals:
        c_back[k].wait_recv()
        c_far[k].wait_recv()
    o[1] = placed(1)
    write_other = pltpu.make_async_copy(o.at[1], out_hbm.at[:, there], local_sem.at[1])
    write_other.start()
    pair.wait_send()
    for group in (y_out, z_out, c_out, z_back, y_back, c_back, c_far):
        for k in group:
            group[k].wait_send()
    write_own.wait()
    write_other.wait()


def on_device(grad_part, seg_slot, owner, left_code, left_scale, right_code, right_scale):
    shards, reps = lax.axis_size("shard"), lax.axis_size("rep")
    assert reps % 4 == 0 and left_code.shape[0] == 2
    if reps > 4:
        every = lax.all_gather(grad_part[0], "rep").astype(F32)
        sums = jnp.sum(every.reshape((reps // 4, 4) + every.shape[1:]), axis=0)
        grad_part = sums[lax.axis_index("rep") % 4][None].astype(BF16)
    _, seg_local, width = grad_part.shape
    half = width // 2
    blocks, order_b = seg_slot.shape
    rows = order_b // shards
    flat = shards * rows
    vmem = pl.BlockSpec(memory_space=pltpu.VMEM)
    hbm = pl.BlockSpec(memory_space=pl.ANY)
    return pl.pallas_call(
        functools.partial(kernel, shards),
        out_shape=jax.ShapeDtypeStruct((seg_local, width), BF16),
        in_specs=[vmem] * 5 + [hbm] * 3,
        out_specs=hbm,
        scratch_shapes=[
            pltpu.VMEM((seg_local, half), BF16),
            pltpu.VMEM((seg_local, half), BF16),
            pltpu.VMEM((2, seg_local, flat), BF16),
            pltpu.VMEM((2, shards, rows, half), BF16),
            pltpu.VMEM((shards, rows, half), BF16),
            pltpu.VMEM((shards, rows, half), BF16),
            pltpu.VMEM((2, shards, rows, half), BF16),
            pltpu.VMEM((order_b, order_b), BF16),
            pltpu.VMEM((2, half, width), BF16),
            pltpu.VMEM((flat, flat), BF16),
            pltpu.VMEM((flat, width), BF16),
            pltpu.VMEM((shards, rows, half), BF16),
            pltpu.VMEM((2, 2, shards, rows, half), BF16),
            pltpu.VMEM((2, seg_local, half), BF16),
            pltpu.SemaphoreType.DMA((6,)),
            pltpu.SemaphoreType.DMA((8, shards)),
            pltpu.SemaphoreType.DMA((8, shards)),
        ],
        compiler_params=pltpu.CompilerParams(
            collective_id=0, has_side_effects=True, vmem_limit_bytes=40 * 1024 * 1024
        ),
    )(seg_slot, owner[:, None], owner[None, :], left_scale, right_scale, grad_part, left_code, right_code)


def solution(mesh):
    in_specs = (
        P("rep", "shard", None),
        P(),
        P(),
        P("shard", None, None),
        P("shard", None),
        P("shard", None, None),
        P("shard", None),
    )
    out_specs = P("shard", None)
    return jax.shard_map(
        on_device, mesh=mesh, in_specs=in_specs, out_specs=out_specs, check_vma=False
    )
```

```python
import functools

import jax
import jax.numpy as jnp
from jax import lax
from jax.experimental import pallas as pl
from jax.experimental.pallas import tpu as pltpu
from jax.sharding import PartitionSpec as P

EPSILON = 1e-06
MESH = pl.DeviceIdType.MESH
F32 = jnp.float32
BF16 = jnp.bfloat16
Y_OUT, Z_OUT, C_OUT, Z_BACK, Y_BACK, C_BACK, C_BACK_FAR, PAIR = range(8)


def log2(value):
    assert value & (value - 1) == 0
    return value.bit_length() - 1


def iota(shape, dim):
    return lax.broadcasted_iota(jnp.int32, shape, dim)


def one_hot(mask):
    return jnp.where(mask, 1.0, 0.0).astype(BF16)


def dot(a, b, contract=((1,), (0,))):
    return lax.dot_general(a, b, (contract, ((), ())), preferred_element_type=F32)


def partner(me, k, shards):
    out = 0
    for j in range(log2(shards)):
        bit = lax.rem(lax.div(me, 1 << j), 2)
        out = out + (1 - bit if (k >> j) & 1 else bit) * (1 << j)
    return out


def send_order(shards):
    far = list(range(shards // 2, shards))
    near = [*range(shards // 4, shards // 2), *range(shards // 4 - 1, 0, -1)]
    order = far[:2]
    for n, k in enumerate(near):
        order += [k] + far[n + 2:n + 3]
    return order


def kernel(
    shards, seg_hbm, owner_hbm, lscale_hbm, rscale_hbm, grad_hbm, left_hbm, right_hbm,
    out_hbm,
    seg_ref, owner_ref, lscale_ref, rscale_ref, p_own, p_got, wt, f, y_got, g, a, left_v, right_v, lperm, mid, u, ud, o, local_sem, send_sem, recv_sem,
):
    rep, me = lax.axis_index("rep"), lax.axis_index("shard")
    y, c = lax.rem(lax.div(rep, 2), 2), lax.rem(rep, 2)
    y_rep, c_rep = rep + 2 - 4 * y, rep + 1 - 2 * c
    blocks, order_b = seg_ref.shape
    rows = order_b // shards
    seg_local, half = p_own.shape
    flat = shards * rows
    order = send_order(shards)
    peers = {k: partner(me, k, shards) for k in order}
    here = pl.ds(pl.multiple_of(c * half, half), half)
    there = pl.ds(pl.multiple_of((1 - c) * half, half), half)

    tables = [
        pltpu.make_async_copy(seg_hbm, seg_ref, local_sem.at[6]),
        pltpu.make_async_copy(owner_hbm, owner_ref, local_sem.at[7]),
    ]
    loads = [
        pltpu.make_async_copy(grad_hbm.at[0, :, here], p_own, local_sem.at[0]),
        pltpu.make_async_copy(left_hbm.at[y], left_v, local_sem.at[1]),
    ]
    for i, r in enumerate((here, there)):
        for j, w in enumerate((here, there)):
            loads.append(pltpu.make_async_copy(
                right_hbm.at[y, r, w], right_v.at[i, :, pl.ds(j * half, half)], local_sem.at[2 + 2 * i + j]))
    loads.append(pltpu.make_async_copy(lscale_hbm, lscale_ref, local_sem.at[8]))
    loads.append(pltpu.make_async_copy(rscale_hbm, rscale_ref, local_sem.at[9]))

    def send(kind, k, src, dst, rep_to, shard_to):
        return pltpu.make_async_remote_copy(
            src_ref=src, dst_ref=dst, send_sem=send_sem.at[kind, k], recv_sem=recv_sem.at[kind, k],
            device_id={"rep": rep_to, "shard": shard_to}, device_id_type=MESH)

    barrier = pltpu.get_barrier_semaphore()
    pl.semaphore_signal(barrier, inc=1, device_id={"rep": c_rep, "shard": me}, device_id_type=MESH)
    pl.semaphore_signal(barrier, inc=1, device_id={"rep": y_rep, "shard": me}, device_id_type=MESH)
    for k in order:
        pl.semaphore_signal(barrier, inc=1, device_id={"rep": rep, "shard": peers[k]}, device_id_type=MESH)
    for load in tables + loads:
        load.start()
    spread = one_hot((iota((order_b, flat), 0) >> log2(shards)) == (iota((order_b, flat), 1) & (rows - 1)))
    pl.semaphore_wait(barrier, 2 + len(order))

    pair = send(PAIR, 0, grad_hbm.at[0, :, there], p_got, c_rep, me)
    pair.start()

    for load in tables:
        load.wait()
    seg = seg_ref[...]
    local = seg - me * seg_local
    local = jnp.where((local >= 0) & (local < seg_local), local, 0)
    digits = jnp.concatenate([local >> 4, local & 15], axis=0).astype(F32).astype(BF16)
    found = dot(digits, spread)
    place_of = found[:blocks] * 16.0 + found[blocks:] + 1.0
    own_row = owner_ref[...].astype(F32)
    line_b, lane_b = iota((blocks, blocks), 0), iota((blocks, blocks), 1)
    own_col = jnp.sum(jnp.where(line_b == lane_b, own_row, 0.0), axis=1, keepdims=True)
    rank = jnp.sum(jnp.where((own_col == own_row) & (lane_b < line_b), 1.0, 0.0), axis=1, keepdims=True)
    key = own_col * 2.0 + rank
    peer_row = (iota((1, flat), 1) >> log2(rows)) ^ me
    seg_id = iota((seg_local, flat), 0).astype(F32)
    for plane in range(2):
        wanted = (peer_row * 2 + lax.rem(y + plane, 2)).astype(F32)
        place = jnp.sum(jnp.where(key == wanted, place_of, 0.0), axis=0, keepdims=True) - 1.0
        wt[plane] = one_hot(seg_id == place)

    loads[0].wait()
    pair.wait_recv()
    q = (p_own[...].astype(F32) + p_got[...].astype(F32)).astype(BF16)
    f[1] = dot(wt[1], q, ((0,), (0,))).astype(BF16).reshape(shards, rows, half)
    y_out = {k: send(Y_OUT, k, f.at[1, k], y_got.at[k], y_rep, me) for k in order + [0]}
    for k in order + [0]:
        y_out[k].start()
    f[0] = dot(wt[0], q, ((0,), (0,))).astype(BF16).reshape(shards, rows, half)
    z_out = {k: send(Z_OUT, k, g.at[k], a.at[0, k], rep, peers[k]) for k in order}
    c_out = {k: send(C_OUT, k, a.at[0, k], a.at[1, k], c_rep, me) for k in order + [0]}

    def pass_on(k):
        y_out[k].wait_recv()
        total = (f[0, k].astype(F32) + y_got[k].astype(F32)).astype(BF16)
        if k:
            g[k] = total
            z_out[k].start()
        else:
            a[0, 0] = total
            c_out[0].start()

    for k in order[:shards // 2]:
        pass_on(k)

    for load in loads[1:]:
        load.wait()
    mine = key == (me * 2 + y).astype(F32)
    first = (seg[:, 0:1] >> log2(seg_local)).astype(F32)
    shift = jnp.sum(jnp.where(mine, first, 0.0), axis=0, keepdims=True).astype(jnp.int32)
    line = iota((flat, 1), 0)
    target = (line & (rows - 1)) * shards + ((((line >> log2(rows)) ^ me) - shift) & (shards - 1))
    chosen = iota((flat, order_b), 1) == target
    lscale = jnp.where(y == 0, lscale_ref[0:1, :], lscale_ref[1:2, :])
    lscale = jnp.sum(jnp.where(chosen, lscale, 0.0), axis=1, keepdims=True)
    rscale = jnp.where(y == 0, rscale_ref[0:1, :], rscale_ref[1:2, :])
    rscale = jnp.where(c == 0, rscale, jnp.concatenate([rscale[:, half:], rscale[:, :half]], axis=1))
    turn = one_hot(chosen)
    lperm[...] = dot(dot(turn, left_v[...]).astype(BF16), turn, ((1,), (1,))).astype(BF16)

    for k in order[shards // 2:] + [0]:
        pass_on(k)
    grad_power = jnp.zeros((1, 1), F32)
    quarter = shards // 4
    waiting = list(order)
    for low, high in ((quarter, 3 * quarter), (0, quarter), (3 * quarter, shards)):
        while any(low <= k < high for k in waiting):
            k = waiting.pop(0)
            z_out[k].wait_recv()
            c_out[k].start()
        for k in range(low, high):
            c_out[k].wait_recv()
        span = (high - low) * rows
        mine_half = a[0, low:high].reshape(span, half)
        other_half = a[1, low:high].reshape(span, half)
        part = dot(mine_half, right_v[0]) + dot(other_half, right_v[1])
        mid[low * rows:high * rows] = (part * rscale).astype(BF16)
        wide, wide_other = mine_half.astype(F32), other_half.astype(F32)
        grad_power += jnp.sum(wide * wide + wide_other * wide_other, keepdims=True)

    precond = dot(lperm[...], mid[...]) * lscale
    update_power = jnp.sum(precond * precond, keepdims=True)
    scale = 1.0 / (order_b * 2 * half)
    ratio = jnp.sqrt((grad_power * scale + EPSILON) / (update_power * scale + EPSILON))
    u[...] = (precond[:, :half] * ratio).astype(BF16).reshape(shards, rows, half)

    z_back = {k: send(Z_BACK, k, u.at[k], ud.at[0, 0, k], rep, peers[k]) for k in order}
    y_back = {k: send(Y_BACK, k, ud.at[0, 0, k], ud.at[1, 0, k], y_rep, me) for k in order + [0]}
    c_back = {k: send(C_BACK, k, ud.at[0, 0, k], ud.at[0, 1, k], c_rep, me) for k in order + [0]}
    c_far = {k: send(C_BACK_FAR, k, ud.at[1, 0, k], ud.at[1, 1, k], c_rep, me) for k in order + [0]}
    for k in order:
        z_back[k].start()
    ud[0, 0, 0] = u[0]
    arrivals = [0] + order
    lag = 3
    for n in range(shards + lag):
        if n < shards:
            k = arrivals[n]
            if k:
                z_back[k].wait_recv()
            y_back[k].start()
            c_back[k].start()
        if n >= lag:
            k = arrivals[n - lag]
            y_back[k].wait_recv()
            c_far[k].start()

    def placed(side):
        return (dot(wt[0], ud[0, side].reshape(flat, half)) + dot(wt[1], ud[1, side].reshape(flat, half))).astype(BF16)

    o[0] = placed(0)
    write_own = pltpu.make_async_copy(o.at[0], out_hbm.at[:, here], local_sem.at[0])
    write_own.start()
    for k in arrivals:
        c_back[k].wait_recv()
        c_far[k].wait_recv()
    o[1] = placed(1)
    write_other = pltpu.make_async_copy(o.at[1], out_hbm.at[:, there], local_sem.at[1])
    write_other.start()
    pair.wait_send()
    for group in (y_out, z_out, c_out, z_back, y_back, c_back, c_far):
        for k in group:
            group[k].wait_send()
    write_own.wait()
    write_other.wait()


def on_device(grad_part, seg_slot, owner, left_code, left_scale, right_code, right_scale):
    shards, reps = lax.axis_size("shard"), lax.axis_size("rep")
    assert reps % 4 == 0 and left_code.shape[0] == 2
    if reps > 4:
        every = lax.all_gather(grad_part[0], "rep").astype(F32)
        sums = jnp.sum(every.reshape((reps // 4, 4) + every.shape[1:]), axis=0)
        grad_part = sums[lax.axis_index("rep") % 4][None].astype(BF16)
    _, seg_local, width = grad_part.shape
    half = width // 2
    blocks, order_b = seg_slot.shape
    rows = order_b // shards
    flat = shards * rows
    hbm = pl.BlockSpec(memory_space=pltpu.HBM)
    return pl.pallas_call(
        functools.partial(kernel, shards),
        out_shape=jax.ShapeDtypeStruct((seg_local, width), BF16),
        in_specs=[hbm] * 7,
        out_specs=hbm,
        scratch_shapes=[
            pltpu.VMEM((blocks, order_b), jnp.int32),
            pltpu.VMEM((1, blocks), jnp.int32),
            pltpu.VMEM((2, order_b), F32),
            pltpu.VMEM((2, width), F32),
            pltpu.VMEM((seg_local, half), BF16),
            pltpu.VMEM((seg_local, half), BF16),
            pltpu.VMEM((2, seg_local, flat), BF16),
            pltpu.VMEM((2, shards, rows, half), BF16),
            pltpu.VMEM((shards, rows, half), BF16),
            pltpu.VMEM((shards, rows, half), BF16),
            pltpu.VMEM((2, shards, rows, half), BF16),
            pltpu.VMEM((order_b, order_b), BF16),
            pltpu.VMEM((2, half, width), BF16),
            pltpu.VMEM((flat, flat), BF16),
            pltpu.VMEM((flat, width), BF16),
            pltpu.VMEM((shards, rows, half), BF16),
            pltpu.VMEM((2, 2, shards, rows, half), BF16),
            pltpu.VMEM((2, seg_local, half), BF16),
            pltpu.SemaphoreType.DMA((10,)),
            pltpu.SemaphoreType.DMA((8, shards)),
            pltpu.SemaphoreType.DMA((8, shards)),
        ],
        compiler_params=pltpu.CompilerParams(
            collective_id=0, has_side_effects=True, vmem_limit_bytes=60 * 1024 * 1024
        ),
    )(seg_slot, owner[None, :], left_scale, right_scale, grad_part, left_code, right_code)


def solution(mesh):
    in_specs = (
        P("rep", "shard", None),
        P(),
        P(),
        P("shard", None, None),
        P("shard", None),
        P("shard", None, None),
        P("shard", None),
    )
    out_specs = P("shard", None)
    return jax.shard_map(
        on_device, mesh=mesh, in_specs=in_specs, out_specs=out_specs, check_vma=False
    )
```

```python
import functools

import jax
import jax.numpy as jnp
from jax import lax
from jax.experimental import pallas as pl
from jax.experimental.pallas import tpu as pltpu
from jax.sharding import PartitionSpec as P

EPSILON = 1e-06
MESH = pl.DeviceIdType.MESH
F32 = jnp.float32
BF16 = jnp.bfloat16
Y_OUT, Z_OUT, C_OUT, Z_BACK, Y_BACK, C_BACK, PAIR = range(7)


def log2(value):
    assert value & (value - 1) == 0
    return value.bit_length() - 1


def iota(shape, dim):
    return lax.broadcasted_iota(jnp.int32, shape, dim)


def one_hot(mask):
    return jnp.where(mask, 1.0, 0.0).astype(BF16)


def dot(a, b, contract=((1,), (0,))):
    return lax.dot_general(a, b, (contract, ((), ())), preferred_element_type=F32)


def partner(me, k, shards):
    out = 0
    for j in range(log2(shards)):
        bit = lax.rem(lax.div(me, 1 << j), 2)
        out = out + (1 - bit if (k >> j) & 1 else bit) * (1 << j)
    return out


def send_order(shards):
    far = list(range(shards // 2, shards))
    near = [*range(shards // 4, shards // 2), *range(shards // 4 - 1, 0, -1)]
    order = far[:2]
    for n, k in enumerate(near):
        order += [k] + far[n + 2:n + 3]
    return order


def kernel(
    shards, seg_hbm, owner_hbm, lscale_hbm, rscale_hbm, grad_hbm, left_hbm, right_hbm,
    own_hbm, other_hbm,
    seg_ref, owner_ref, lscale_ref, rscale_ref, p_own, p_got, wt, f, y_got, g, a, left_v, right_v, lperm, mid, u, ud, acc, done, local_sem, send_sem, recv_sem,
):
    rep, me = lax.axis_index("rep"), lax.axis_index("shard")
    y, c = lax.rem(lax.div(rep, 2), 2), lax.rem(rep, 2)
    y_rep, c_rep = rep + 2 - 4 * y, rep + 1 - 2 * c
    blocks, order_b = seg_ref.shape
    rows = order_b // shards
    seg_local, half = p_own.shape
    flat = shards * rows
    order = send_order(shards)
    peers = {k: partner(me, k, shards) for k in order}
    here = pl.ds(pl.multiple_of(c * half, half), half)
    there = pl.ds(pl.multiple_of((1 - c) * half, half), half)

    tables = [
        pltpu.make_async_copy(seg_hbm, seg_ref, local_sem.at[6]),
        pltpu.make_async_copy(owner_hbm, owner_ref, local_sem.at[7]),
    ]
    loads = [
        pltpu.make_async_copy(grad_hbm.at[0, :, here], p_own, local_sem.at[0]),
        pltpu.make_async_copy(left_hbm.at[y], left_v, local_sem.at[1]),
    ]
    for i, r in enumerate((here, there)):
        for j, w in enumerate((here, there)):
            loads.append(pltpu.make_async_copy(
                right_hbm.at[y, r, w], right_v.at[i, :, pl.ds(j * half, half)], local_sem.at[2 + 2 * i + j]))
    loads.append(pltpu.make_async_copy(lscale_hbm, lscale_ref, local_sem.at[8]))
    loads.append(pltpu.make_async_copy(rscale_hbm, rscale_ref, local_sem.at[9]))

    def send(kind, k, src, dst, rep_to, shard_to):
        return pltpu.make_async_remote_copy(
            src_ref=src, dst_ref=dst, send_sem=send_sem.at[kind, k], recv_sem=recv_sem.at[kind, k],
            device_id={"rep": rep_to, "shard": shard_to}, device_id_type=MESH)

    barrier = pltpu.get_barrier_semaphore()
    pl.semaphore_signal(barrier, inc=1, device_id={"rep": c_rep, "shard": me}, device_id_type=MESH)
    pl.semaphore_signal(barrier, inc=1, device_id={"rep": y_rep, "shard": me}, device_id_type=MESH)
    for k in order:
        pl.semaphore_signal(barrier, inc=1, device_id={"rep": rep, "shard": peers[k]}, device_id_type=MESH)
    for load in tables + loads:
        load.start()
    spread = one_hot((iota((order_b, flat), 0) >> log2(shards)) == (iota((order_b, flat), 1) & (rows - 1)))
    pl.semaphore_wait(barrier, 2 + len(order))

    pair = send(PAIR, 0, grad_hbm.at[0, :, there], p_got, c_rep, me)
    pair.start()

    for load in tables:
        load.wait()
    seg = seg_ref[...]
    local = seg - me * seg_local
    local = jnp.where((local >= 0) & (local < seg_local), local, 0)
    digits = jnp.concatenate([local >> 4, local & 15], axis=0).astype(F32).astype(BF16)
    found = dot(digits, spread)
    place_of = found[:blocks] * 16.0 + found[blocks:] + 1.0
    own_row = owner_ref[...].astype(F32)
    line_b, lane_b = iota((blocks, blocks), 0), iota((blocks, blocks), 1)
    own_col = jnp.sum(jnp.where(line_b == lane_b, own_row, 0.0), axis=1, keepdims=True)
    rank = jnp.sum(jnp.where((own_col == own_row) & (lane_b < line_b), 1.0, 0.0), axis=1, keepdims=True)
    key = own_col * 2.0 + rank
    peer_row = (iota((1, flat), 1) >> log2(rows)) ^ me
    seg_id = iota((seg_local, flat), 0).astype(F32)
    for plane in range(2):
        wanted = (peer_row * 2 + lax.rem(y + plane, 2)).astype(F32)
        place = jnp.sum(jnp.where(key == wanted, place_of, 0.0), axis=0, keepdims=True) - 1.0
        wt[plane] = one_hot(seg_id == place)

    loads[0].wait()
    pair.wait_recv()
    q = (p_own[...].astype(F32) + p_got[...].astype(F32)).astype(BF16)
    f[1] = dot(wt[1], q, ((0,), (0,))).astype(BF16).reshape(shards, rows, half)
    y_out = {k: send(Y_OUT, k, f.at[1, k], y_got.at[k], y_rep, me) for k in order + [0]}
    for k in order + [0]:
        y_out[k].start()
    f[0] = dot(wt[0], q, ((0,), (0,))).astype(BF16).reshape(shards, rows, half)
    z_out = {k: send(Z_OUT, k, g.at[k], a.at[0, k], rep, peers[k]) for k in order}
    quarter = shards // 4
    spans = ((quarter, 3 * quarter), (0, quarter), (3 * quarter, shards))
    c_out = {
        n: send(C_OUT, n, a.at[0, low:high], a.at[1, low:high], c_rep, me) for n, (low, high) in enumerate(spans)
    }

    def pass_on(k):
        y_out[k].wait_recv()
        total = (f[0, k].astype(F32) + y_got[k].astype(F32)).astype(BF16)
        if k:
            g[k] = total
            z_out[k].start()
        else:
            a[0, 0] = total

    for k in order[:shards // 2]:
        pass_on(k)

    for load in loads[1:]:
        load.wait()
    mine = key == (me * 2 + y).astype(F32)
    first = (seg[:, 0:1] >> log2(seg_local)).astype(F32)
    shift = jnp.sum(jnp.where(mine, first, 0.0), axis=0, keepdims=True).astype(jnp.int32)
    line = iota((flat, 1), 0)
    target = (line & (rows - 1)) * shards + ((((line >> log2(rows)) ^ me) - shift) & (shards - 1))
    chosen = iota((flat, order_b), 1) == target
    lscale = jnp.where(y == 0, lscale_ref[0:1, :], lscale_ref[1:2, :])
    lscale = jnp.sum(jnp.where(chosen, lscale, 0.0), axis=1, keepdims=True)
    rscale = jnp.where(y == 0, rscale_ref[0:1, :], rscale_ref[1:2, :])
    rscale = jnp.where(c == 0, rscale, jnp.concatenate([rscale[:, half:], rscale[:, :half]], axis=1))
    turn = one_hot(chosen)
    lperm[...] = dot(dot(turn, left_v[...]).astype(BF16), turn, ((1,), (1,))).astype(BF16)

    for k in order[shards // 2:] + [0]:
        pass_on(k)
    grad_power = jnp.zeros((1, 1), F32)
    waiting = list(order)
    for n, (low, high) in enumerate(spans):
        while any(low <= k < high for k in waiting):
            z_out[waiting.pop(0)].wait_recv()
        c_out[n].start()
    for n, (low, high) in enumerate(spans):
        c_out[n].wait_recv()
        span = (high - low) * rows
        mine_half = a[0, low:high].reshape(span, half)
        other_half = a[1, low:high].reshape(span, half)
        part = dot(mine_half, right_v[0]) + dot(other_half, right_v[1])
        mid[low * rows:high * rows] = (part * rscale).astype(BF16)
        wide, wide_other = mine_half.astype(F32), other_half.astype(F32)
        grad_power += jnp.sum(wide * wide + wide_other * wide_other, keepdims=True)

    precond = dot(lperm[...], mid[...]) * lscale
    update_power = jnp.sum(precond * precond, keepdims=True)
    scale = 1.0 / (order_b * 2 * half)
    ratio = jnp.sqrt((grad_power * scale + EPSILON) / (update_power * scale + EPSILON))
    u[...] = (precond[:, :half] * ratio).astype(BF16).reshape(shards, rows, half)

    z_back = {k: send(Z_BACK, k, u.at[k], ud.at[0, k], rep, peers[k]) for k in order}
    y_back = {k: send(Y_BACK, k, ud.at[0, k], ud.at[1, k], y_rep, me) for k in order + [0]}
    for k in order:
        z_back[k].start()
    ud[0, 0] = u[0]
    y_back[0].start()
    for k in order:
        z_back[k].wait_recv()
        y_back[k].start()

    def placed(at, low, high):
        lanes = slice(low * rows, high * rows)
        span = (high - low) * rows
        return sum(dot(wt[n, at, lanes], ud[n, low:high].reshape(span, half)) for n in range(2))

    waiting = [0] + order
    low, high = spans[0]
    while any(low <= k < high for k in waiting):
        y_back[waiting.pop(0)].wait_recv()
    acc[...] = placed(slice(None), low, high)
    for k in waiting:
        y_back[k].wait_recv()
    c_back, writes = {}, []
    for n in range(2):
        at = slice(n * seg_local // 2, (n + 1) * seg_local // 2)
        done[at] = (acc[at] + placed(at, *spans[1]) + placed(at, *spans[2])).astype(BF16)
        c_back[n] = send(C_BACK, n, done.at[at], other_hbm.at[at], c_rep, me)
        c_back[n].start()
        writes.append(pltpu.make_async_copy(done.at[at], own_hbm.at[at], local_sem.at[n]))
        writes[n].start()
    for n in c_back:
        c_back[n].wait_recv()
    pair.wait_send()
    for group in (y_out, z_out, c_out, z_back, y_back, c_back):
        for k in group:
            group[k].wait_send()
    for write in writes:
        write.wait()


def on_device(grad_part, seg_slot, owner, left_code, left_scale, right_code, right_scale):
    shards, reps = lax.axis_size("shard"), lax.axis_size("rep")
    assert reps % 4 == 0 and left_code.shape[0] == 2
    if reps > 4:
        every = lax.all_gather(grad_part[0], "rep").astype(F32)
        sums = jnp.sum(every.reshape((reps // 4, 4) + every.shape[1:]), axis=0)
        grad_part = sums[lax.axis_index("rep") % 4][None].astype(BF16)
    _, seg_local, width = grad_part.shape
    half = width // 2
    blocks, order_b = seg_slot.shape
    rows = order_b // shards
    flat = shards * rows
    hbm = pl.BlockSpec(memory_space=pltpu.HBM)
    own, other = pl.pallas_call(
        functools.partial(kernel, shards),
        out_shape=[jax.ShapeDtypeStruct((seg_local, half), BF16)] * 2,
        in_specs=[hbm] * 7,
        out_specs=[hbm, hbm],
        scratch_shapes=[
            pltpu.VMEM((blocks, order_b), jnp.int32),
            pltpu.VMEM((1, blocks), jnp.int32),
            pltpu.VMEM((2, order_b), F32),
            pltpu.VMEM((2, width), F32),
            pltpu.VMEM((seg_local, half), BF16),
            pltpu.VMEM((seg_local, half), BF16),
            pltpu.VMEM((2, seg_local, flat), BF16),
            pltpu.VMEM((2, shards, rows, half), BF16),
            pltpu.VMEM((shards, rows, half), BF16),
            pltpu.VMEM((shards, rows, half), BF16),
            pltpu.VMEM((2, shards, rows, half), BF16),
            pltpu.VMEM((order_b, order_b), BF16),
            pltpu.VMEM((2, half, width), BF16),
            pltpu.VMEM((flat, flat), BF16),
            pltpu.VMEM((flat, width), BF16),
            pltpu.VMEM((shards, rows, half), BF16),
            pltpu.VMEM((2, shards, rows, half), BF16),
            pltpu.VMEM((seg_local, half), F32),
            pltpu.VMEM((seg_local, half), BF16),
            pltpu.SemaphoreType.DMA((10,)),
            pltpu.SemaphoreType.DMA((7, shards)),
            pltpu.SemaphoreType.DMA((7, shards)),
        ],
        compiler_params=pltpu.CompilerParams(
            collective_id=0, has_side_effects=True, vmem_limit_bytes=60 * 1024 * 1024
        ),
    )(seg_slot, owner[None, :], left_scale, right_scale, grad_part, left_code, right_code)
    first = (lax.axis_index("rep") & 1) == 0
    return jnp.concatenate([jnp.where(first, own, other), jnp.where(first, other, own)], axis=1)


def solution(mesh):
    in_specs = (
        P("rep", "shard", None),
        P(),
        P(),
        P("shard", None, None),
        P("shard", None),
        P("shard", None, None),
        P("shard", None),
    )
    out_specs = P("shard", None)
    return jax.shard_map(
        on_device, mesh=mesh, in_specs=in_specs, out_specs=out_specs, check_vma=False
    )
```

```python
import functools

import jax
import jax.numpy as jnp
from jax import lax
from jax.experimental import pallas as pl
from jax.experimental.pallas import tpu as pltpu
from jax.sharding import PartitionSpec as P

EPSILON = 1e-06
MESH = pl.DeviceIdType.MESH
F32 = jnp.float32
BF16 = jnp.bfloat16
Y_OUT, Z_OUT, C_OUT, Z_BACK, Y_BACK, C_BACK, PAIR = range(7)
JOINS = 4


def log2(value):
    assert value & (value - 1) == 0
    return value.bit_length() - 1


def iota(shape, dim):
    return lax.broadcasted_iota(jnp.int32, shape, dim)


def one_hot(mask):
    return jnp.where(mask, 1.0, 0.0).astype(BF16)


def dot(a, b, contract=((1,), (0,))):
    return lax.dot_general(a, b, (contract, ((), ())), preferred_element_type=F32)


def partner(me, k, shards):
    out = 0
    for j in range(log2(shards)):
        bit = lax.rem(lax.div(me, 1 << j), 2)
        out = out + (1 - bit if (k >> j) & 1 else bit) * (1 << j)
    return out


def send_order(shards):
    far = list(range(shards // 2, shards))
    near = [*range(shards // 4, shards // 2), *range(shards // 4 - 1, 0, -1)]
    order = far[:2]
    for n, k in enumerate(near):
        order += [k] + far[n + 2:n + 3]
    return order


def kernel(
    shards, seg_hbm, owner_hbm, lscale_hbm, rscale_hbm, grad_hbm, left_hbm, right_hbm,
    own_hbm, other_hbm,
    seg_ref, owner_ref, lscale_ref, rscale_ref, p_own, p_got, wt, f, y_got, g, a, left_v, right_v, lperm, mid, u, ud, acc, done, local_sem, send_sem, recv_sem,
):
    rep, me = lax.axis_index("rep"), lax.axis_index("shard")
    y, c = lax.rem(lax.div(rep, 2), 2), lax.rem(rep, 2)
    y_rep, c_rep = rep + 2 - 4 * y, rep + 1 - 2 * c
    blocks, order_b = seg_ref.shape
    rows = order_b // shards
    seg_local, half = p_own.shape
    flat = shards * rows
    order = send_order(shards)
    peers = {k: partner(me, k, shards) for k in order}
    here = pl.ds(pl.multiple_of(c * half, half), half)
    there = pl.ds(pl.multiple_of((1 - c) * half, half), half)

    tables = [
        pltpu.make_async_copy(seg_hbm, seg_ref, local_sem.at[6]),
        pltpu.make_async_copy(owner_hbm, owner_ref, local_sem.at[7]),
    ]
    loads = [
        pltpu.make_async_copy(grad_hbm.at[0, :, here], p_own, local_sem.at[0]),
        pltpu.make_async_copy(left_hbm.at[y], left_v, local_sem.at[1]),
    ]
    for i, r in enumerate((here, there)):
        for j, w in enumerate((here, there)):
            loads.append(pltpu.make_async_copy(
                right_hbm.at[y, r, w], right_v.at[i, :, pl.ds(j * half, half)], local_sem.at[2 + 2 * i + j]))
    loads.append(pltpu.make_async_copy(lscale_hbm, lscale_ref, local_sem.at[8]))
    loads.append(pltpu.make_async_copy(rscale_hbm, rscale_ref, local_sem.at[9]))

    def send(kind, k, src, dst, rep_to, shard_to):
        return pltpu.make_async_remote_copy(
            src_ref=src, dst_ref=dst, send_sem=send_sem.at[kind, k], recv_sem=recv_sem.at[kind, k],
            device_id={"rep": rep_to, "shard": shard_to}, device_id_type=MESH)

    barrier = pltpu.get_barrier_semaphore()
    pl.semaphore_signal(barrier, inc=1, device_id={"rep": c_rep, "shard": me}, device_id_type=MESH)
    pl.semaphore_signal(barrier, inc=1, device_id={"rep": y_rep, "shard": me}, device_id_type=MESH)
    for k in order:
        pl.semaphore_signal(barrier, inc=1, device_id={"rep": rep, "shard": peers[k]}, device_id_type=MESH)
    for load in tables + loads:
        load.start()
    gather = one_hot((iota((flat, order_b), 1) >> log2(shards)) == (iota((flat, order_b), 0) & (rows - 1)))
    pl.semaphore_wait(barrier, 2 + len(order))

    pair = send(PAIR, 0, grad_hbm.at[0, :, there], p_got, c_rep, me)
    pair.start()

    for load in tables:
        load.wait()
    seg = seg_ref[...]
    local = seg - me * seg_local
    local = jnp.where((local >= 0) & (local < seg_local), local, 0)
    digits = jnp.concatenate([local >> 4, local & 15], axis=0).astype(F32).astype(BF16)
    found = dot(gather, digits, ((1,), (1,)))
    place_of = found[:, :blocks] * 16.0 + found[:, blocks:] + 1.0
    own_row = owner_ref[...].astype(F32)
    line_b, lane_b = iota((blocks, blocks), 0), iota((blocks, blocks), 1)
    own_col = jnp.sum(jnp.where(line_b == lane_b, own_row, 0.0), axis=1, keepdims=True)
    same = own_col == own_row
    key_row = own_row * 2.0 + jnp.sum(jnp.where(same & (line_b < lane_b), 1.0, 0.0), axis=0, keepdims=True)
    key = own_col * 2.0 + jnp.sum(jnp.where(same & (lane_b < line_b), 1.0, 0.0), axis=1, keepdims=True)
    peer_col = (iota((flat, 1), 0) >> log2(rows)) ^ me
    seg_lane = iota((flat, seg_local), 1).astype(F32)

    def picked(plane):
        wanted = (peer_col * 2 + lax.rem(y + plane, 2)).astype(F32)
        place = jnp.sum(jnp.where(key_row == wanted, place_of, 0.0), axis=1, keepdims=True) - 1.0
        return one_hot(seg_lane == place)

    pick_far = picked(1)
    loads[0].wait()
    pair.wait_recv()
    q = (p_own[...].astype(F32) + p_got[...].astype(F32)).astype(BF16)
    f[1] = dot(pick_far, q).astype(BF16).reshape(shards, rows, half)
    y_out = {k: send(Y_OUT, k, f.at[1, k], y_got.at[k], y_rep, me) for k in order + [0]}
    for k in order + [0]:
        y_out[k].start()
    f[0] = dot(picked(0), q).astype(BF16).reshape(shards, rows, half)
    z_out = {k: send(Z_OUT, k, g.at[k], a.at[0, k], rep, peers[k]) for k in order}
    quarter = shards // 4
    spans = ((quarter, 3 * quarter), (0, quarter), (3 * quarter, shards))
    c_out = {
        n: send(C_OUT, n, a.at[0, low:high], a.at[1, low:high], c_rep, me) for n, (low, high) in enumerate(spans)
    }

    def pass_on(k):
        y_out[k].wait_recv()
        total = (f[0, k].astype(F32) + y_got[k].astype(F32)).astype(BF16)
        if k:
            g[k] = total
            z_out[k].start()
        else:
            a[0, 0] = total

    for k in order[:shards // 2]:
        pass_on(k)

    spread = one_hot((iota((order_b, flat), 0) >> log2(shards)) == (iota((order_b, flat), 1) & (rows - 1)))
    found = dot(digits, spread)
    place_of = found[:blocks] * 16.0 + found[blocks:] + 1.0
    peer_row = (iota((1, flat), 1) >> log2(rows)) ^ me
    seg_id = iota((seg_local, flat), 0).astype(F32)
    for plane in range(2):
        wanted = (peer_row * 2 + lax.rem(y + plane, 2)).astype(F32)
        place = jnp.sum(jnp.where(key == wanted, place_of, 0.0), axis=0, keepdims=True) - 1.0
        wt[plane] = one_hot(seg_id == place)

    for load in loads[1:]:
        load.wait()
    mine = key == (me * 2 + y).astype(F32)
    first = (seg[:, 0:1] >> log2(seg_local)).astype(F32)
    shift = jnp.sum(jnp.where(mine, first, 0.0), axis=0, keepdims=True).astype(jnp.int32)
    line = iota((flat, 1), 0)
    target = (line & (rows - 1)) * shards + ((((line >> log2(rows)) ^ me) - shift) & (shards - 1))
    chosen = iota((flat, order_b), 1) == target
    lscale = jnp.where(y == 0, lscale_ref[0:1, :], lscale_ref[1:2, :])
    lscale = jnp.sum(jnp.where(chosen, lscale, 0.0), axis=1, keepdims=True)
    rscale = jnp.where(y == 0, rscale_ref[0:1, :], rscale_ref[1:2, :])
    rscale = jnp.where(c == 0, rscale, jnp.concatenate([rscale[:, half:], rscale[:, :half]], axis=1))
    turn = one_hot(chosen)
    lperm[...] = dot(dot(turn, left_v[...]).astype(BF16), turn, ((1,), (1,))).astype(BF16)

    for k in order[shards // 2:] + [0]:
        pass_on(k)
    late = order[:-2] + [order[-1], order[-2]]
    waiting = list(late)

    def middle(n):
        low, high = spans[n]
        c_out[n].wait_recv()
        span = (high - low) * rows
        mine_half = a[0, low:high].reshape(span, half)
        other_half = a[1, low:high].reshape(span, half)
        part = dot(mine_half, right_v[0]) + dot(other_half, right_v[1])
        mid[low * rows:high * rows] = (part * rscale).astype(BF16)
        wide, wide_other = mine_half.astype(F32), other_half.astype(F32)
        return jnp.sum(wide * wide + wide_other * wide_other, keepdims=True)

    grad_power = jnp.zeros((1, 1), F32)
    for n, (low, high) in enumerate(spans):
        while any(low <= k < high for k in waiting):
            z_out[waiting.pop(0)].wait_recv()
        c_out[n].start()
        if n:
            grad_power += middle(n - 1)
    grad_power += middle(len(spans) - 1)

    precond = dot(lperm[...], mid[...]) * lscale
    update_power = jnp.sum(precond * precond, keepdims=True)
    scale = 1.0 / (order_b * 2 * half)
    ratio = jnp.sqrt((grad_power * scale + EPSILON) / (update_power * scale + EPSILON))
    u[...] = (precond[:, :half] * ratio).astype(BF16).reshape(shards, rows, half)

    z_back = {k: send(Z_BACK, k, u.at[k], ud.at[0, k], rep, peers[k]) for k in order}
    y_back = {k: send(Y_BACK, k, ud.at[0, k], ud.at[1, k], y_rep, me) for k in order + [0]}
    for k in order:
        z_back[k].start()
    ud[0, 0] = u[0]
    y_back[0].start()
    for k in late:
        z_back[k].wait_recv()
        y_back[k].start()

    def placed(at, low, high):
        lanes = slice(low * rows, high * rows)
        span = (high - low) * rows
        return sum(dot(wt[n, at, lanes], ud[n, low:high].reshape(span, half)) for n in range(2))

    waiting = [0] + late
    low, high = spans[0]
    while any(low <= k < high for k in waiting):
        y_back[waiting.pop(0)].wait_recv()
    acc[...] = placed(slice(None), low, high)
    for k in waiting:
        y_back[k].wait_recv()
    c_back, writes = {}, []
    for n in range(2):
        at = slice(n * seg_local // 2, (n + 1) * seg_local // 2)
        done[at] = (acc[at] + placed(at, *spans[1]) + placed(at, *spans[2])).astype(BF16)
        c_back[n] = send(C_BACK, n, done.at[at], other_hbm.at[at], c_rep, me)
        c_back[n].start()
        writes.append(pltpu.make_async_copy(done.at[at], own_hbm.at[at], local_sem.at[n]))
        writes[n].start()
    for n in c_back:
        c_back[n].wait_recv()
    pair.wait_send()
    for group in (y_out, z_out, c_out, z_back, y_back, c_back):
        for k in group:
            group[k].wait_send()
    for write in writes:
        write.wait()


def join(own_hbm, other_hbm, out_hbm, sem):
    c = lax.rem(lax.axis_index("rep"), 2)
    seg_local, half = own_hbm.shape
    step = seg_local // JOINS
    copies = []
    for n, (ref, side) in enumerate(((own_hbm, c), (other_hbm, 1 - c))):
        lanes = pl.ds(pl.multiple_of(side * half, half), half)
        for i in range(JOINS):
            at = pl.ds(i * step, step)
            copies.append(pltpu.make_async_copy(ref.at[at], out_hbm.at[at, lanes], sem.at[n, i]))
    for copy in copies:
        copy.start()
    for copy in copies:
        copy.wait()


def on_device(grad_part, seg_slot, owner, left_code, left_scale, right_code, right_scale):
    shards, reps = lax.axis_size("shard"), lax.axis_size("rep")
    assert reps % 4 == 0 and left_code.shape[0] == 2
    if reps > 4:
        every = lax.all_gather(grad_part[0], "rep").astype(F32)
        sums = jnp.sum(every.reshape((reps // 4, 4) + every.shape[1:]), axis=0)
        grad_part = sums[lax.axis_index("rep") % 4][None].astype(BF16)
    _, seg_local, width = grad_part.shape
    half = width // 2
    blocks, order_b = seg_slot.shape
    rows = order_b // shards
    flat = shards * rows
    hbm = pl.BlockSpec(memory_space=pltpu.HBM)
    own, other = pl.pallas_call(
        functools.partial(kernel, shards),
        out_shape=[jax.ShapeDtypeStruct((seg_local, half), BF16)] * 2,
        in_specs=[hbm] * 7,
        out_specs=[hbm, hbm],
        scratch_shapes=[
            pltpu.VMEM((blocks, order_b), jnp.int32),
            pltpu.VMEM((1, blocks), jnp.int32),
            pltpu.VMEM((2, order_b), F32),
            pltpu.VMEM((2, width), F32),
            pltpu.VMEM((seg_local, half), BF16),
            pltpu.VMEM((seg_local, half), BF16),
            pltpu.VMEM((2, seg_local, flat), BF16),
            pltpu.VMEM((2, shards, rows, half), BF16),
            pltpu.VMEM((shards, rows, half), BF16),
            pltpu.VMEM((shards, rows, half), BF16),
            pltpu.VMEM((2, shards, rows, half), BF16),
            pltpu.VMEM((order_b, order_b), BF16),
            pltpu.VMEM((2, half, width), BF16),
            pltpu.VMEM((flat, flat), BF16),
            pltpu.VMEM((flat, width), BF16),
            pltpu.VMEM((shards, rows, half), BF16),
            pltpu.VMEM((2, shards, rows, half), BF16),
            pltpu.VMEM((seg_local, half), F32),
            pltpu.VMEM((seg_local, half), BF16),
            pltpu.SemaphoreType.DMA((10,)),
            pltpu.SemaphoreType.DMA((7, shards)),
            pltpu.SemaphoreType.DMA((7, shards)),
        ],
        compiler_params=pltpu.CompilerParams(
            collective_id=0, has_side_effects=True, vmem_limit_bytes=60 * 1024 * 1024
        ),
    )(seg_slot, owner[None, :], left_scale, right_scale, grad_part, left_code, right_code)
    return pl.pallas_call(
        join,
        out_shape=jax.ShapeDtypeStruct((seg_local, width), BF16),
        in_specs=[hbm, hbm],
        out_specs=hbm,
        scratch_shapes=[pltpu.SemaphoreType.DMA((2, JOINS))],
        compiler_params=pltpu.CompilerParams(vmem_limit_bytes=60 * 1024 * 1024),
    )(own, other)


def solution(mesh):
    in_specs = (
        P("rep", "shard", None),
        P(),
        P(),
        P("shard", None, None),
        P("shard", None),
        P("shard", None, None),
        P("shard", None),
    )
    out_specs = P("shard", None)
    return jax.shard_map(
        on_device, mesh=mesh, in_specs=in_specs, out_specs=out_specs, check_vma=False
    )
```

```python
import functools

import jax
import jax.numpy as jnp
from jax import lax
from jax.experimental import pallas as pl
from jax.experimental.pallas import tpu as pltpu
from jax.sharding import PartitionSpec as P

EPSILON = 1e-06
MESH = pl.DeviceIdType.MESH
F32 = jnp.float32
BF16 = jnp.bfloat16
Y_OUT, Z_OUT, C_OUT, Z_BACK, Y_BACK, C_BACK, PAIR = range(7)
JOINS = 4


def log2(value):
    assert value & (value - 1) == 0
    return value.bit_length() - 1


def iota(shape, dim):
    return lax.broadcasted_iota(jnp.int32, shape, dim)


def one_hot(mask):
    return jnp.where(mask, 1.0, 0.0).astype(BF16)


def dot(a, b, contract=((1,), (0,))):
    return lax.dot_general(a, b, (contract, ((), ())), preferred_element_type=F32)


def partner(me, k, shards):
    out = 0
    for j in range(log2(shards)):
        bit = lax.rem(lax.div(me, 1 << j), 2)
        out = out + (1 - bit if (k >> j) & 1 else bit) * (1 << j)
    return out


def send_order(shards):
    far = list(range(shards // 2, shards))
    near = [*range(shards // 4, shards // 2), *range(shards // 4 - 1, 0, -1)]
    order = far[:2]
    for n, k in enumerate(near):
        order += [k] + far[n + 2:n + 3]
    return order


def kernel(
    shards, seg_hbm, owner_hbm, lscale_hbm, rscale_hbm, grad_hbm, left_hbm, right_hbm,
    own_hbm, other_hbm,
    seg_ref, owner_ref, lscale_ref, rscale_ref, p_own, p_got, wt, f, y_got, g, a, left_v, right_v, lperm, mid, u, ud, acc, done, local_sem, send_sem, recv_sem,
):
    rep, me = lax.axis_index("rep"), lax.axis_index("shard")
    y, c = lax.rem(lax.div(rep, 2), 2), lax.rem(rep, 2)
    y_rep, c_rep = rep + 2 - 4 * y, rep + 1 - 2 * c
    blocks, order_b = seg_ref.shape
    rows = order_b // shards
    seg_local, half = p_own.shape
    flat = shards * rows
    order = send_order(shards)
    peers = {k: partner(me, k, shards) for k in order}
    here = pl.ds(pl.multiple_of(c * half, half), half)
    there = pl.ds(pl.multiple_of((1 - c) * half, half), half)

    tables = [
        pltpu.make_async_copy(seg_hbm, seg_ref, local_sem.at[6]),
        pltpu.make_async_copy(owner_hbm, owner_ref, local_sem.at[7]),
    ]
    loads = [
        pltpu.make_async_copy(grad_hbm.at[0, :, here], p_own, local_sem.at[0]),
        pltpu.make_async_copy(left_hbm.at[y], left_v, local_sem.at[1]),
    ]
    for i, r in enumerate((here, there)):
        for j, w in enumerate((here, there)):
            loads.append(pltpu.make_async_copy(
                right_hbm.at[y, r, w], right_v.at[i, :, pl.ds(j * half, half)], local_sem.at[2 + 2 * i + j]))
    loads.append(pltpu.make_async_copy(lscale_hbm, lscale_ref, local_sem.at[8]))
    loads.append(pltpu.make_async_copy(rscale_hbm, rscale_ref, local_sem.at[9]))

    def send(kind, k, src, dst, rep_to, shard_to):
        return pltpu.make_async_remote_copy(
            src_ref=src, dst_ref=dst, send_sem=send_sem.at[kind, k], recv_sem=recv_sem.at[kind, k],
            device_id={"rep": rep_to, "shard": shard_to}, device_id_type=MESH)

    for load in tables + loads[:1]:
        load.start()
    barrier = pltpu.get_barrier_semaphore()
    pl.semaphore_signal(barrier, inc=1, device_id={"rep": c_rep, "shard": me}, device_id_type=MESH)
    pl.semaphore_signal(barrier, inc=1, device_id={"rep": y_rep, "shard": me}, device_id_type=MESH)
    for k in order:
        pl.semaphore_signal(barrier, inc=1, device_id={"rep": rep, "shard": peers[k]}, device_id_type=MESH)
    pl.semaphore_wait(barrier, 2 + len(order))

    pair = send(PAIR, 0, grad_hbm.at[0, :, there], p_got, c_rep, me)
    pair.start()
    for load in loads[1:]:
        load.start()
    gather = one_hot((iota((flat, order_b), 1) >> log2(shards)) == (iota((flat, order_b), 0) & (rows - 1)))

    for load in tables:
        load.wait()
    seg = seg_ref[...]
    local = seg - me * seg_local
    local = jnp.where((local >= 0) & (local < seg_local), local, 0)
    digits = jnp.concatenate([local >> 4, local & 15], axis=0).astype(F32).astype(BF16)
    found = dot(gather, digits, ((1,), (1,)))
    place_of = found[:, :blocks] * 16.0 + found[:, blocks:] + 1.0
    own_row = owner_ref[...].astype(F32)
    line_b, lane_b = iota((blocks, blocks), 0), iota((blocks, blocks), 1)
    own_col = jnp.sum(jnp.where(line_b == lane_b, own_row, 0.0), axis=1, keepdims=True)
    same = own_col == own_row
    key_row = own_row * 2.0 + jnp.sum(jnp.where(same & (line_b < lane_b), 1.0, 0.0), axis=0, keepdims=True)
    key = own_col * 2.0 + jnp.sum(jnp.where(same & (lane_b < line_b), 1.0, 0.0), axis=1, keepdims=True)
    peer_col = (iota((flat, 1), 0) >> log2(rows)) ^ me
    seg_lane = iota((flat, seg_local), 1).astype(F32)

    def picked(plane):
        wanted = (peer_col * 2 + lax.rem(y + plane, 2)).astype(F32)
        place = jnp.sum(jnp.where(key_row == wanted, place_of, 0.0), axis=1, keepdims=True) - 1.0
        return one_hot(seg_lane == place)

    pick_far = picked(1)
    loads[0].wait()
    pair.wait_recv()
    q = (p_own[...].astype(F32) + p_got[...].astype(F32)).astype(BF16)
    f[1] = dot(pick_far, q).astype(BF16).reshape(shards, rows, half)
    y_out = {k: send(Y_OUT, k, f.at[1, k], y_got.at[k], y_rep, me) for k in order + [0]}
    for k in order + [0]:
        y_out[k].start()
    f[0] = dot(picked(0), q).astype(BF16).reshape(shards, rows, half)
    z_out = {k: send(Z_OUT, k, g.at[k], a.at[0, k], rep, peers[k]) for k in order}
    quarter = shards // 4
    spans = ((quarter, 3 * quarter), (0, quarter), (3 * quarter, shards))
    c_out = {
        n: send(C_OUT, n, a.at[0, low:high], a.at[1, low:high], c_rep, me) for n, (low, high) in enumerate(spans)
    }

    def pass_on(k):
        y_out[k].wait_recv()
        total = (f[0, k].astype(F32) + y_got[k].astype(F32)).astype(BF16)
        if k:
            g[k] = total
            z_out[k].start()
        else:
            a[0, 0] = total

    for k in order[:-1]:
        pass_on(k)

    for load in loads[1:]:
        load.wait()
    mine = key == (me * 2 + y).astype(F32)
    first = (seg[:, 0:1] >> log2(seg_local)).astype(F32)
    shift = jnp.sum(jnp.where(mine, first, 0.0), axis=0, keepdims=True).astype(jnp.int32)
    line = iota((flat, 1), 0)
    target = (line & (rows - 1)) * shards + ((((line >> log2(rows)) ^ me) - shift) & (shards - 1))
    chosen = iota((flat, order_b), 1) == target
    lscale = jnp.where(y == 0, lscale_ref[0:1, :], lscale_ref[1:2, :])
    lscale = jnp.sum(jnp.where(chosen, lscale, 0.0), axis=1, keepdims=True)
    rscale = jnp.where(y == 0, rscale_ref[0:1, :], rscale_ref[1:2, :])
    rscale = jnp.where(c == 0, rscale, jnp.concatenate([rscale[:, half:], rscale[:, :half]], axis=1))
    turn = one_hot(chosen)
    lperm[...] = dot(dot(turn, left_v[...]).astype(BF16), turn, ((1,), (1,))).astype(BF16)

    for k in order[-1:] + [0]:
        pass_on(k)
    late = order[:-2] + [order[-1], order[-2]]
    early = [order[2], order[0]] + sorted(set(range(1, shards // 2)) - {order[2]}, reverse=True) + order[1:2]
    early += sorted(set(range(shards // 2, shards)) - set(order[:2]))
    waiting = list(late)

    def middle(n):
        low, high = spans[n]
        c_out[n].wait_recv()
        span = (high - low) * rows
        mine_half = a[0, low:high].reshape(span, half)
        other_half = a[1, low:high].reshape(span, half)
        part = dot(mine_half, right_v[0]) + dot(other_half, right_v[1])
        mid[low * rows:high * rows] = (part * rscale).astype(BF16)
        wide, wide_other = mine_half.astype(F32), other_half.astype(F32)
        return jnp.sum(wide * wide + wide_other * wide_other, keepdims=True)

    grad_power = jnp.zeros((1, 1), F32)
    for n, (low, high) in enumerate(spans):
        while any(low <= k < high for k in waiting):
            z_out[waiting.pop(0)].wait_recv()
        c_out[n].start()
        if n:
            grad_power += middle(n - 1)
    grad_power += middle(len(spans) - 1)

    precond = dot(lperm[...], mid[...]) * lscale
    update_power = jnp.sum(precond * precond, keepdims=True)
    scale = 1.0 / (order_b * 2 * half)
    ratio = jnp.sqrt((grad_power * scale + EPSILON) / (update_power * scale + EPSILON))
    u[...] = (precond[:, :half] * ratio).astype(BF16).reshape(shards, rows, half)

    z_back = {k: send(Z_BACK, k, u.at[k], ud.at[0, k], rep, peers[k]) for k in order}
    y_back = {k: send(Y_BACK, k, ud.at[0, k], ud.at[1, k], y_rep, me) for k in order + [0]}
    for k in order:
        z_back[k].start()
    ud[0, 0] = u[0]
    y_back[0].start()
    spread = one_hot((iota((order_b, flat), 0) >> log2(shards)) == (iota((order_b, flat), 1) & (rows - 1)))
    found = dot(digits, spread)
    place_of = found[:blocks] * 16.0 + found[blocks:] + 1.0
    peer_row = (iota((1, flat), 1) >> log2(rows)) ^ me
    seg_id = iota((seg_local, flat), 0).astype(F32)
    for plane in range(2):
        wanted = (peer_row * 2 + lax.rem(y + plane, 2)).astype(F32)
        place = jnp.sum(jnp.where(key == wanted, place_of, 0.0), axis=0, keepdims=True) - 1.0
        wt[plane] = one_hot(seg_id == place)
    for k in early:
        z_back[k].wait_recv()
        y_back[k].start()

    def placed(at, low, high):
        lanes = slice(low * rows, high * rows)
        span = (high - low) * rows
        return sum(dot(wt[n, at, lanes], ud[n, low:high].reshape(span, half)) for n in range(2))

    waiting = [0] + early
    low, high = spans[0]
    while any(low <= k < high for k in waiting):
        y_back[waiting.pop(0)].wait_recv()
    acc[...] = placed(slice(None), low, high)
    for k in waiting:
        y_back[k].wait_recv()
    c_back, writes = {}, []
    for n in range(2):
        at = slice(n * seg_local // 2, (n + 1) * seg_local // 2)
        done[at] = (acc[at] + placed(at, *spans[1]) + placed(at, *spans[2])).astype(BF16)
        c_back[n] = send(C_BACK, n, done.at[at], other_hbm.at[at], c_rep, me)
        c_back[n].start()
        writes.append(pltpu.make_async_copy(done.at[at], own_hbm.at[at], local_sem.at[n]))
        writes[n].start()
    for n in c_back:
        c_back[n].wait_recv()
    pair.wait_send()
    for group in (y_out, z_out, c_out, z_back, y_back, c_back):
        for k in group:
            group[k].wait_send()
    for write in writes:
        write.wait()


def join(own_hbm, other_hbm, out_hbm, whole, in_sem, out_sem):
    c = lax.rem(lax.axis_index("rep"), 2)
    seg_local, half = own_hbm.shape
    step = seg_local // JOINS
    reads, writes = [], []
    for i in range(JOINS):
        at = pl.ds(i * step, step)
        for n, (ref, side) in enumerate(((own_hbm, c), (other_hbm, 1 - c))):
            lanes = pl.ds(pl.multiple_of(side * half, half), half)
            reads.append(pltpu.make_async_copy(ref.at[at], whole.at[at, lanes], in_sem.at[n, i]))
            reads[-1].start()
    for i in range(JOINS):
        at = pl.ds(i * step, step)
        reads[2 * i].wait()
        reads[2 * i + 1].wait()
        writes.append(pltpu.make_async_copy(whole.at[at], out_hbm.at[at], out_sem.at[i]))
        writes[-1].start()
    for write in writes:
        write.wait()


def on_device(grad_part, seg_slot, owner, left_code, left_scale, right_code, right_scale):
    shards, reps = lax.axis_size("shard"), lax.axis_size("rep")
    assert reps % 4 == 0 and left_code.shape[0] == 2
    if reps > 4:
        every = lax.all_gather(grad_part[0], "rep").astype(F32)
        sums = jnp.sum(every.reshape((reps // 4, 4) + every.shape[1:]), axis=0)
        grad_part = sums[lax.axis_index("rep") % 4][None].astype(BF16)
    _, seg_local, width = grad_part.shape
    half = width // 2
    blocks, order_b = seg_slot.shape
    rows = order_b // shards
    flat = shards * rows
    hbm = pl.BlockSpec(memory_space=pltpu.HBM)
    own, other = pl.pallas_call(
        functools.partial(kernel, shards),
        out_shape=[jax.ShapeDtypeStruct((seg_local, half), BF16)] * 2,
        in_specs=[hbm] * 7,
        out_specs=[hbm, hbm],
        scratch_shapes=[
            pltpu.VMEM((blocks, order_b), jnp.int32),
            pltpu.VMEM((1, blocks), jnp.int32),
            pltpu.VMEM((2, order_b), F32),
            pltpu.VMEM((2, width), F32),
            pltpu.VMEM((seg_local, half), BF16),
            pltpu.VMEM((seg_local, half), BF16),
            pltpu.VMEM((2, seg_local, flat), BF16),
            pltpu.VMEM((2, shards, rows, half), BF16),
            pltpu.VMEM((shards, rows, half), BF16),
            pltpu.VMEM((shards, rows, half), BF16),
            pltpu.VMEM((2, shards, rows, half), BF16),
            pltpu.VMEM((order_b, order_b), BF16),
            pltpu.VMEM((2, half, width), BF16),
            pltpu.VMEM((flat, flat), BF16),
            pltpu.VMEM((flat, width), BF16),
            pltpu.VMEM((shards, rows, half), BF16),
            pltpu.VMEM((2, shards, rows, half), BF16),
            pltpu.VMEM((seg_local, half), F32),
            pltpu.VMEM((seg_local, half), BF16),
            pltpu.SemaphoreType.DMA((10,)),
            pltpu.SemaphoreType.DMA((7, shards)),
            pltpu.SemaphoreType.DMA((7, shards)),
        ],
        compiler_params=pltpu.CompilerParams(
            collective_id=0, has_side_effects=True, vmem_limit_bytes=60 * 1024 * 1024
        ),
    )(seg_slot, owner[None, :], left_scale, right_scale, grad_part, left_code, right_code)
    return pl.pallas_call(
        join,
        out_shape=jax.ShapeDtypeStruct((seg_local, width), BF16),
        in_specs=[hbm, hbm],
        out_specs=hbm,
        scratch_shapes=[
            pltpu.VMEM((seg_local, width), BF16),
            pltpu.SemaphoreType.DMA((2, JOINS)),
            pltpu.SemaphoreType.DMA((JOINS,)),
        ],
        compiler_params=pltpu.CompilerParams(vmem_limit_bytes=60 * 1024 * 1024),
    )(own, other)


def solution(mesh):
    in_specs = (
        P("rep", "shard", None),
        P(),
        P(),
        P("shard", None, None),
        P("shard", None),
        P("shard", None, None),
        P("shard", None),
    )
    out_specs = P("shard", None)
    return jax.shard_map(
        on_device, mesh=mesh, in_specs=in_specs, out_specs=out_specs, check_vma=False
    )
```

```python
import functools

import jax
import jax.numpy as jnp
from jax import lax
from jax.experimental import pallas as pl
from jax.experimental.pallas import tpu as pltpu
from jax.sharding import PartitionSpec as P

EPSILON = 1e-06
MESH = pl.DeviceIdType.MESH
F32 = jnp.float32
BF16 = jnp.bfloat16
Y_OUT, Z_OUT, C_OUT, Z_BACK, Y_BACK, C_BACK, PAIR = range(7)
JOINS = 4


def log2(value):
    assert value & (value - 1) == 0
    return value.bit_length() - 1


def iota(shape, dim):
    return lax.broadcasted_iota(jnp.int32, shape, dim)


def one_hot(mask):
    return jnp.where(mask, 1.0, 0.0).astype(BF16)


def dot(a, b, contract=((1,), (0,))):
    return lax.dot_general(a, b, (contract, ((), ())), preferred_element_type=F32)


def partner(me, k, shards):
    out = 0
    for j in range(log2(shards)):
        bit = lax.rem(lax.div(me, 1 << j), 2)
        out = out + (1 - bit if (k >> j) & 1 else bit) * (1 << j)
    return out


def send_order(shards):
    mid = shards // 2
    order = []
    for n in range(1, mid):
        order += [mid + n, mid - n]
    return order


def kernel(
    shards, seg_hbm, owner_hbm, lscale_hbm, rscale_hbm, grad_hbm, left_hbm, right_hbm,
    own_hbm, other_hbm,
    seg_ref, owner_ref, lscale_ref, rscale_ref, p_own, p_got, wt, f, y_got, g, a, left_v, right_v, lperm, mid, u, ud, acc, done, local_sem, send_sem, recv_sem,
):
    rep, me = lax.axis_index("rep"), lax.axis_index("shard")
    y, c = lax.rem(lax.div(rep, 2), 2), lax.rem(rep, 2)
    y_rep, c_rep = rep + 2 - 4 * y, rep + 1 - 2 * c
    blocks, order_b = seg_ref.shape
    rows = order_b // shards
    seg_local, half = p_own.shape
    flat = shards * rows
    mid_label = shards // 2
    flipped = partner(me, mid_label, shards)
    origin = me + c * (flipped - me)
    own, mate = c * mid_label, (1 - c) * mid_label
    order = send_order(shards)
    peers = {k: partner(origin, k, shards) for k in order}
    order = ["mate"] + order
    label = {"mate": mate, "own": own, **{k: k for k in peers}}
    peers["mate"] = flipped
    here = pl.ds(pl.multiple_of(c * half, half), half)
    there = pl.ds(pl.multiple_of((1 - c) * half, half), half)

    tables = [
        pltpu.make_async_copy(seg_hbm, seg_ref, local_sem.at[6]),
        pltpu.make_async_copy(owner_hbm, owner_ref, local_sem.at[7]),
    ]
    loads = [
        pltpu.make_async_copy(grad_hbm.at[0, :, here], p_own, local_sem.at[0]),
        pltpu.make_async_copy(left_hbm.at[y], left_v, local_sem.at[1]),
    ]
    for i, r in enumerate((here, there)):
        for j, w in enumerate((here, there)):
            loads.append(pltpu.make_async_copy(
                right_hbm.at[y, r, w], right_v.at[i, :, pl.ds(j * half, half)], local_sem.at[2 + 2 * i + j]))
    loads.append(pltpu.make_async_copy(lscale_hbm, lscale_ref, local_sem.at[8]))
    loads.append(pltpu.make_async_copy(rscale_hbm, rscale_ref, local_sem.at[9]))

    def send(kind, k, src, dst, rep_to, shard_to):
        k = label.get(k, k)
        return pltpu.make_async_remote_copy(
            src_ref=src, dst_ref=dst, send_sem=send_sem.at[kind, k], recv_sem=recv_sem.at[kind, k],
            device_id={"rep": rep_to, "shard": shard_to}, device_id_type=MESH)

    for load in tables + loads[:1]:
        load.start()
    barrier = pltpu.get_barrier_semaphore()
    pl.semaphore_signal(barrier, inc=1, device_id={"rep": c_rep, "shard": me}, device_id_type=MESH)
    pl.semaphore_signal(barrier, inc=1, device_id={"rep": y_rep, "shard": me}, device_id_type=MESH)
    for k in order:
        pl.semaphore_signal(barrier, inc=1, device_id={"rep": rep, "shard": peers[k]}, device_id_type=MESH)
    pl.semaphore_wait(barrier, 2 + len(order))

    pair = send(PAIR, 0, grad_hbm.at[0, :, there], p_got, c_rep, me)
    pair.start()
    for load in loads[1:]:
        load.start()
    gather = one_hot((iota((flat, order_b), 1) >> log2(shards)) == (iota((flat, order_b), 0) & (rows - 1)))

    for load in tables:
        load.wait()
    seg = seg_ref[...]
    local = seg - me * seg_local
    local = jnp.where((local >= 0) & (local < seg_local), local, 0)
    digits = jnp.concatenate([local >> 4, local & 15], axis=0).astype(F32).astype(BF16)
    found = dot(gather, digits, ((1,), (1,)))
    place_of = found[:, :blocks] * 16.0 + found[:, blocks:] + 1.0
    own_row = owner_ref[...].astype(F32)
    line_b, lane_b = iota((blocks, blocks), 0), iota((blocks, blocks), 1)
    own_col = jnp.sum(jnp.where(line_b == lane_b, own_row, 0.0), axis=1, keepdims=True)
    same = own_col == own_row
    key_row = own_row * 2.0 + jnp.sum(jnp.where(same & (line_b < lane_b), 1.0, 0.0), axis=0, keepdims=True)
    key = own_col * 2.0 + jnp.sum(jnp.where(same & (lane_b < line_b), 1.0, 0.0), axis=1, keepdims=True)
    peer_col = (iota((flat, 1), 0) >> log2(rows)) ^ origin
    seg_lane = iota((flat, seg_local), 1).astype(F32)

    def picked(plane):
        wanted = (peer_col * 2 + lax.rem(y + plane, 2)).astype(F32)
        place = jnp.sum(jnp.where(key_row == wanted, place_of, 0.0), axis=1, keepdims=True) - 1.0
        return one_hot(seg_lane == place)

    pick_far = picked(1)
    loads[0].wait()
    pair.wait_recv()
    q = (p_own[...].astype(F32) + p_got[...].astype(F32)).astype(BF16)
    f[1] = dot(pick_far, q).astype(BF16).reshape(shards, rows, half)
    y_out = {k: send(Y_OUT, k, f.at[1, label[k]], y_got.at[label[k]], y_rep, me) for k in order + ["own"]}
    for k in order + ["own"]:
        y_out[k].start()
    f[0] = dot(picked(0), q).astype(BF16).reshape(shards, rows, half)
    z_out = {k: send(Z_OUT, k, g.at[label[k]], a.at[0, label[k]], rep, peers[k]) for k in order}
    quarter = shards // 4
    spans = ((2 * quarter, 3 * quarter), (quarter, 2 * quarter), (3 * quarter, shards), (0, quarter))
    c_out = {}
    for n, (low, high) in enumerate(spans):
        to = (low + mid_label) % shards
        c_out[n] = send(C_OUT, n, a.at[0, low:high], a.at[1, to:to + quarter], c_rep, me)

    def pass_on(k):
        y_out[k].wait_recv()
        at = label[k]
        total = (f[0, at].astype(F32) + y_got[at].astype(F32)).astype(BF16)
        if k != "own":
            g[at] = total
            z_out[k].start()
        else:
            a[0, own] = total

    for k in order[:-1]:
        pass_on(k)

    for load in loads[1:]:
        load.wait()
    mine = key == (me * 2 + y).astype(F32)
    first = (seg[:, 0:1] >> log2(seg_local)).astype(F32)
    shift = jnp.sum(jnp.where(mine, first, 0.0), axis=0, keepdims=True).astype(jnp.int32)
    line = iota((flat, 1), 0)
    target = (line & (rows - 1)) * shards + ((((line >> log2(rows)) ^ origin) - shift) & (shards - 1))
    chosen = iota((flat, order_b), 1) == target
    lscale = jnp.where(y == 0, lscale_ref[0:1, :], lscale_ref[1:2, :])
    lscale = jnp.sum(jnp.where(chosen, lscale, 0.0), axis=1, keepdims=True)
    rscale = jnp.where(y == 0, rscale_ref[0:1, :], rscale_ref[1:2, :])
    rscale = jnp.where(c == 0, rscale, jnp.concatenate([rscale[:, half:], rscale[:, :half]], axis=1))
    turn = one_hot(chosen)
    lperm[...] = dot(dot(turn, left_v[...]).astype(BF16), turn, ((1,), (1,))).astype(BF16)

    for k in order[-1:] + ["own"]:
        pass_on(k)
    waiting = list(order)

    def middle(n):
        low, high = spans[n]
        span = (high - low) * rows
        mine_half = a[0, low:high].reshape(span, half)
        other_half = a[1, low:high].reshape(span, half)
        part = dot(mine_half, right_v[0]) + dot(other_half, right_v[1])
        mid[low * rows:high * rows] = (part * rscale).astype(BF16)
        wide, wide_other = mine_half.astype(F32), other_half.astype(F32)
        return jnp.sum(wide * wide + wide_other * wide_other, keepdims=True)

    landed = [(n, next(m for m, (low, _) in enumerate(spans) if low == (spans[n][0] + mid_label) % shards))
              for n in range(len(spans))]
    grad_power = jnp.zeros((1, 1), F32)
    started = set()
    received = set()
    for n, (low, high) in enumerate(spans):
        while any(low <= k < high for k in waiting if k != "mate") or "mate" in waiting:
            z_out[waiting.pop(0)].wait_recv()
        c_out[n].start()
        started.add(n)
        if n:
            c_out[n - 1].wait_recv()
            received.add(n - 1)
        for here_n, from_n in landed:
            if here_n in started and from_n in received:
                grad_power += middle(here_n)
                started.remove(here_n)
    c_out[len(spans) - 1].wait_recv()
    received.add(len(spans) - 1)
    for here_n, from_n in landed:
        if here_n in started:
            grad_power += middle(here_n)

    precond = dot(lperm[...], mid[...]) * lscale
    update_power = jnp.sum(precond * precond, keepdims=True)
    scale = 1.0 / (order_b * 2 * half)
    ratio = jnp.sqrt((grad_power * scale + EPSILON) / (update_power * scale + EPSILON))
    u[...] = (precond[:, :half] * ratio).astype(BF16).reshape(shards, rows, half)

    z_back = {k: send(Z_BACK, k, u.at[label[k]], ud.at[0, label[k]], rep, peers[k]) for k in order}
    y_back = {k: send(Y_BACK, k, ud.at[0, label[k]], ud.at[1, label[k]], y_rep, me) for k in order + ["own"]}
    for k in order:
        z_back[k].start()
    ud[0, own] = u[own]
    y_back["own"].start()
    spread = one_hot((iota((order_b, flat), 0) >> log2(shards)) == (iota((order_b, flat), 1) & (rows - 1)))
    found = dot(digits, spread)
    place_of = found[:blocks] * 16.0 + found[blocks:] + 1.0
    peer_row = (iota((1, flat), 1) >> log2(rows)) ^ origin
    seg_id = iota((seg_local, flat), 0).astype(F32)
    for plane in range(2):
        wanted = (peer_row * 2 + lax.rem(y + plane, 2)).astype(F32)
        place = jnp.sum(jnp.where(key == wanted, place_of, 0.0), axis=0, keepdims=True) - 1.0
        wt[plane] = one_hot(seg_id == place)
    for k in order:
        z_back[k].wait_recv()
        y_back[k].start()

    def placed(at, low, high):
        lanes = slice(low * rows, high * rows)
        span = (high - low) * rows
        return sum(dot(wt[n, at, lanes], ud[n, low:high].reshape(span, half)) for n in range(2))

    waiting = ["own"] + order
    while any(k in waiting for k in ["mate"] + [k for k in order[1:] if quarter <= k < 3 * quarter]):
        y_back[waiting.pop(0)].wait_recv()
    acc[...] = placed(slice(None), quarter, 3 * quarter)
    for k in waiting:
        y_back[k].wait_recv()
    c_back, writes = {}, []
    for n in range(2):
        at = slice(n * seg_local // 2, (n + 1) * seg_local // 2)
        done[at] = (acc[at] + placed(at, 0, quarter) + placed(at, 3 * quarter, shards)).astype(BF16)
        c_back[n] = send(C_BACK, n, done.at[at], other_hbm.at[at], c_rep, me)
        c_back[n].start()
        writes.append(pltpu.make_async_copy(done.at[at], own_hbm.at[at], local_sem.at[n]))
        writes[n].start()
    for n in c_back:
        c_back[n].wait_recv()
    pair.wait_send()
    for group in (y_out, z_out, c_out, z_back, y_back, c_back):
        for k in group:
            group[k].wait_send()
    for write in writes:
        write.wait()


def join(own_hbm, other_hbm, out_hbm, whole, in_sem, out_sem):
    c = lax.rem(lax.axis_index("rep"), 2)
    seg_local, half = own_hbm.shape
    step = seg_local // JOINS
    reads, writes = [], []
    for i in range(JOINS):
        at = pl.ds(i * step, step)
        for n, (ref, side) in enumerate(((own_hbm, c), (other_hbm, 1 - c))):
            lanes = pl.ds(pl.multiple_of(side * half, half), half)
            reads.append(pltpu.make_async_copy(ref.at[at], whole.at[at, lanes], in_sem.at[n, i]))
            reads[-1].start()
    for i in range(JOINS):
        at = pl.ds(i * step, step)
        reads[2 * i].wait()
        reads[2 * i + 1].wait()
        writes.append(pltpu.make_async_copy(whole.at[at], out_hbm.at[at], out_sem.at[i]))
        writes[-1].start()
    for write in writes:
        write.wait()


def on_device(grad_part, seg_slot, owner, left_code, left_scale, right_code, right_scale):
    shards, reps = lax.axis_size("shard"), lax.axis_size("rep")
    assert reps % 4 == 0 and left_code.shape[0] == 2
    if reps > 4:
        every = lax.all_gather(grad_part[0], "rep").astype(F32)
        sums = jnp.sum(every.reshape((reps // 4, 4) + every.shape[1:]), axis=0)
        grad_part = sums[lax.axis_index("rep") % 4][None].astype(BF16)
    _, seg_local, width = grad_part.shape
    half = width // 2
    blocks, order_b = seg_slot.shape
    rows = order_b // shards
    flat = shards * rows
    hbm = pl.BlockSpec(memory_space=pltpu.HBM)
    own, other = pl.pallas_call(
        functools.partial(kernel, shards),
        out_shape=[jax.ShapeDtypeStruct((seg_local, half), BF16)] * 2,
        in_specs=[hbm] * 7,
        out_specs=[hbm, hbm],
        scratch_shapes=[
            pltpu.VMEM((blocks, order_b), jnp.int32),
            pltpu.VMEM((1, blocks), jnp.int32),
            pltpu.VMEM((2, order_b), F32),
            pltpu.VMEM((2, width), F32),
            pltpu.VMEM((seg_local, half), BF16),
            pltpu.VMEM((seg_local, half), BF16),
            pltpu.VMEM((2, seg_local, flat), BF16),
            pltpu.VMEM((2, shards, rows, half), BF16),
            pltpu.VMEM((shards, rows, half), BF16),
            pltpu.VMEM((shards, rows, half), BF16),
            pltpu.VMEM((2, shards, rows, half), BF16),
            pltpu.VMEM((order_b, order_b), BF16),
            pltpu.VMEM((2, half, width), BF16),
            pltpu.VMEM((flat, flat), BF16),
            pltpu.VMEM((flat, width), BF16),
            pltpu.VMEM((shards, rows, half), BF16),
            pltpu.VMEM((2, shards, rows, half), BF16),
            pltpu.VMEM((seg_local, half), F32),
            pltpu.VMEM((seg_local, half), BF16),
            pltpu.SemaphoreType.DMA((10,)),
            pltpu.SemaphoreType.DMA((7, shards)),
            pltpu.SemaphoreType.DMA((7, shards)),
        ],
        compiler_params=pltpu.CompilerParams(
            collective_id=0, has_side_effects=True, vmem_limit_bytes=60 * 1024 * 1024
        ),
    )(seg_slot, owner[None, :], left_scale, right_scale, grad_part, left_code, right_code)
    return pl.pallas_call(
        join,
        out_shape=jax.ShapeDtypeStruct((seg_local, width), BF16),
        in_specs=[hbm, hbm],
        out_specs=hbm,
        scratch_shapes=[
            pltpu.VMEM((seg_local, width), BF16),
            pltpu.SemaphoreType.DMA((2, JOINS)),
            pltpu.SemaphoreType.DMA((JOINS,)),
        ],
        compiler_params=pltpu.CompilerParams(vmem_limit_bytes=60 * 1024 * 1024),
    )(own, other)


def solution(mesh):
    in_specs = (
        P("rep", "shard", None),
        P(),
        P(),
        P("shard", None, None),
        P("shard", None),
        P("shard", None, None),
        P("shard", None),
    )
    out_specs = P("shard", None)
    return jax.shard_map(
        on_device, mesh=mesh, in_specs=in_specs, out_specs=out_specs, check_vma=False
    )
```

```python
import functools

import jax
import jax.numpy as jnp
from jax import lax
from jax.experimental import pallas as pl
from jax.experimental.pallas import tpu as pltpu
from jax.sharding import PartitionSpec as P

EPSILON = 1e-06
MESH = pl.DeviceIdType.MESH
F32 = jnp.float32
BF16 = jnp.bfloat16
Y_OUT, Z_OUT, C_OUT, Z_BACK, Y_BACK, C_BACK, PAIR = range(7)
JOINS = 2


def log2(value):
    assert value & (value - 1) == 0
    return value.bit_length() - 1


def iota(shape, dim):
    return lax.broadcasted_iota(jnp.int32, shape, dim)


def one_hot(mask):
    return jnp.where(mask, 1.0, 0.0).astype(BF16)


def dot(a, b, contract=((1,), (0,))):
    return lax.dot_general(a, b, (contract, ((), ())), preferred_element_type=F32)


def partner(me, k, shards):
    out = 0
    for j in range(log2(shards)):
        bit = lax.rem(lax.div(me, 1 << j), 2)
        out = out + (1 - bit if (k >> j) & 1 else bit) * (1 << j)
    return out


def send_order(shards):
    far = list(range(shards // 2, shards))
    near = [*range(shards // 4, shards // 2), *range(shards // 4 - 1, 0, -1)]
    order = far[:2]
    for n, k in enumerate(near):
        order += [k] + far[n + 2:n + 3]
    return order


def kernel(
    shards, seg_hbm, owner_hbm, lscale_hbm, rscale_hbm, grad_hbm, left_hbm, right_hbm,
    own_hbm, other_hbm,
    seg_ref, owner_ref, lscale_ref, rscale_ref, p_own, p_got, wt, f, y_got, g, a, left_v, right_v, lperm, mid, partial, u, ud, acc, done, local_sem, send_sem, recv_sem,
):
    rep, me = lax.axis_index("rep"), lax.axis_index("shard")
    y, c = lax.rem(lax.div(rep, 2), 2), lax.rem(rep, 2)
    y_rep, c_rep = rep + 2 - 4 * y, rep + 1 - 2 * c
    blocks, order_b = seg_ref.shape
    rows = order_b // shards
    seg_local, half = p_own.shape
    flat = shards * rows
    order = send_order(shards)
    peers = {k: partner(me, k, shards) for k in order}
    here = pl.ds(pl.multiple_of(c * half, half), half)
    there = pl.ds(pl.multiple_of((1 - c) * half, half), half)

    tables = [
        pltpu.make_async_copy(seg_hbm, seg_ref, local_sem.at[6]),
        pltpu.make_async_copy(owner_hbm, owner_ref, local_sem.at[7]),
    ]
    loads = [
        pltpu.make_async_copy(grad_hbm.at[0, :, here], p_own, local_sem.at[0]),
        pltpu.make_async_copy(left_hbm.at[y], left_v, local_sem.at[1]),
    ]
    for i, r in enumerate((here, there)):
        for j, w in enumerate((here, there)):
            loads.append(pltpu.make_async_copy(
                right_hbm.at[y, r, w], right_v.at[i, :, pl.ds(j * half, half)], local_sem.at[2 + 2 * i + j]))
    loads.append(pltpu.make_async_copy(lscale_hbm, lscale_ref, local_sem.at[8]))
    loads.append(pltpu.make_async_copy(rscale_hbm, rscale_ref, local_sem.at[9]))

    def send(kind, k, src, dst, rep_to, shard_to):
        return pltpu.make_async_remote_copy(
            src_ref=src, dst_ref=dst, send_sem=send_sem.at[kind, k], recv_sem=recv_sem.at[kind, k],
            device_id={"rep": rep_to, "shard": shard_to}, device_id_type=MESH)

    for load in tables + loads[:1]:
        load.start()
    barrier = pltpu.get_barrier_semaphore()
    pl.semaphore_signal(barrier, inc=1, device_id={"rep": c_rep, "shard": me}, device_id_type=MESH)
    pl.semaphore_signal(barrier, inc=1, device_id={"rep": y_rep, "shard": me}, device_id_type=MESH)
    for k in order:
        pl.semaphore_signal(barrier, inc=1, device_id={"rep": rep, "shard": peers[k]}, device_id_type=MESH)
    pl.semaphore_wait(barrier, 2 + len(order))

    pair = send(PAIR, 0, grad_hbm.at[0, :, there], p_got, c_rep, me)
    pair.start()
    for load in loads[1:]:
        load.start()
    gather = one_hot((iota((flat, order_b), 1) >> log2(shards)) == (iota((flat, order_b), 0) & (rows - 1)))

    for load in tables:
        load.wait()
    seg = seg_ref[...]
    local = seg - me * seg_local
    local = jnp.where((local >= 0) & (local < seg_local), local, 0)
    digits = jnp.concatenate([local >> 4, local & 15], axis=0).astype(F32).astype(BF16)
    found = dot(gather, digits, ((1,), (1,)))
    place_of = found[:, :blocks] * 16.0 + found[:, blocks:] + 1.0
    own_row = owner_ref[...].astype(F32)
    line_b, lane_b = iota((blocks, blocks), 0), iota((blocks, blocks), 1)
    own_col = jnp.sum(jnp.where(line_b == lane_b, own_row, 0.0), axis=1, keepdims=True)
    same = own_col == own_row
    key_row = own_row * 2.0 + jnp.sum(jnp.where(same & (line_b < lane_b), 1.0, 0.0), axis=0, keepdims=True)
    key = own_col * 2.0 + jnp.sum(jnp.where(same & (lane_b < line_b), 1.0, 0.0), axis=1, keepdims=True)
    peer_col = (iota((flat, 1), 0) >> log2(rows)) ^ me
    seg_lane = iota((flat, seg_local), 1).astype(F32)

    def picked(plane):
        wanted = (peer_col * 2 + lax.rem(y + plane, 2)).astype(F32)
        place = jnp.sum(jnp.where(key_row == wanted, place_of, 0.0), axis=1, keepdims=True) - 1.0
        return one_hot(seg_lane == place)

    pick_far = picked(1)
    loads[0].wait()
    pair.wait_recv()
    q = (p_own[...].astype(F32) + p_got[...].astype(F32)).astype(BF16)
    quarter = shards // 4
    spans = ((quarter, 3 * quarter), (0, quarter), (3 * quarter, shards))
    y_out = {k: send(Y_OUT, k, f.at[1, k], y_got.at[k], y_rep, me) for k in order + [0]}
    unsent = order + [0]
    for n, (low, high) in enumerate(spans):
        part = dot(pick_far[low * rows:high * rows], q)
        f[1, low:high] = part.astype(BF16).reshape(high - low, rows, half)
        while unsent and n == 0 and low <= unsent[0] < high:
            y_out[unsent.pop(0)].start()
    for k in unsent:
        y_out[k].start()
    f[0] = dot(picked(0), q).astype(BF16).reshape(shards, rows, half)
    z_out = {k: send(Z_OUT, k, g.at[k], a.at[0, k], rep, peers[k]) for k in order}
    c_out = {
        n: send(C_OUT, n, a.at[0, low:high], a.at[1, low:high], c_rep, me) for n, (low, high) in enumerate(spans)
    }

    def pass_on(k):
        y_out[k].wait_recv()
        total = (f[0, k].astype(F32) + y_got[k].astype(F32)).astype(BF16)
        if k:
            g[k] = total
            z_out[k].start()
        else:
            a[0, 0] = total

    for k in order[:-1]:
        pass_on(k)

    for load in loads[1:]:
        load.wait()
    mine = key == (me * 2 + y).astype(F32)
    first = (seg[:, 0:1] >> log2(seg_local)).astype(F32)
    shift = jnp.sum(jnp.where(mine, first, 0.0), axis=0, keepdims=True).astype(jnp.int32)
    line = iota((flat, 1), 0)
    target = (line & (rows - 1)) * shards + ((((line >> log2(rows)) ^ me) - shift) & (shards - 1))
    chosen = iota((flat, order_b), 1) == target
    lscale = jnp.where(y == 0, lscale_ref[0:1, :], lscale_ref[1:2, :])
    lscale = jnp.sum(jnp.where(chosen, lscale, 0.0), axis=1, keepdims=True)
    rscale = jnp.where(y == 0, rscale_ref[0:1, :], rscale_ref[1:2, :])
    rscale = jnp.where(c == 0, rscale, jnp.concatenate([rscale[:, half:], rscale[:, :half]], axis=1))
    turn = one_hot(chosen)
    lperm[...] = dot(dot(turn, left_v[...]).astype(BF16), turn, ((1,), (1,))).astype(BF16)

    for k in order[-1:] + [0]:
        pass_on(k)
    late = order[:-2] + [order[-1], order[-2]]
    early = [order[2], order[0]] + sorted(set(range(1, shards // 2)) - {order[2]}, reverse=True) + order[1:2]
    early += sorted(set(range(shards // 2, shards)) - set(order[:2]))
    waiting = list(late)

    def middle(n):
        low, high = spans[n]
        c_out[n].wait_recv()
        span = (high - low) * rows
        mine_half = a[0, low:high].reshape(span, half)
        other_half = a[1, low:high].reshape(span, half)
        part = dot(mine_half, right_v[0]) + dot(other_half, right_v[1])
        mid[low * rows:high * rows] = (part * rscale).astype(BF16)
        wide, wide_other = mine_half.astype(F32), other_half.astype(F32)
        return jnp.sum(wide * wide + wide_other * wide_other, keepdims=True)

    grad_power = jnp.zeros((1, 1), F32)
    for n, (low, high) in enumerate(spans):
        while any(low <= k < high for k in waiting):
            z_out[waiting.pop(0)].wait_recv()
        c_out[n].start()
        if n:
            grad_power += middle(n - 1)
    known = 3 * quarter * rows
    partial[...] = dot(lperm[:, :known], mid[:known])
    grad_power += middle(len(spans) - 1)

    precond = (partial[...] + dot(lperm[:, known:], mid[known:])) * lscale
    update_power = jnp.sum(precond * precond, keepdims=True)
    scale = 1.0 / (order_b * 2 * half)
    ratio = jnp.sqrt((grad_power * scale + EPSILON) / (update_power * scale + EPSILON))
    u[...] = (precond[:, :half] * ratio).astype(BF16).reshape(shards, rows, half)

    z_back = {k: send(Z_BACK, k, u.at[k], ud.at[0, k], rep, peers[k]) for k in order}
    y_back = {k: send(Y_BACK, k, ud.at[0, k], ud.at[1, k], y_rep, me) for k in order + [0]}
    for k in order:
        z_back[k].start()
    ud[0, 0] = u[0]
    y_back[0].start()
    spread = one_hot((iota((order_b, flat), 0) >> log2(shards)) == (iota((order_b, flat), 1) & (rows - 1)))
    found = dot(digits, spread)
    place_of = found[:blocks] * 16.0 + found[blocks:] + 1.0
    peer_row = (iota((1, flat), 1) >> log2(rows)) ^ me
    seg_id = iota((seg_local, flat), 0).astype(F32)
    for plane in range(2):
        wanted = (peer_row * 2 + lax.rem(y + plane, 2)).astype(F32)
        place = jnp.sum(jnp.where(key == wanted, place_of, 0.0), axis=0, keepdims=True) - 1.0
        wt[plane] = one_hot(seg_id == place)
    for k in early:
        z_back[k].wait_recv()
        y_back[k].start()

    def placed(at, low, high):
        lanes = slice(low * rows, high * rows)
        span = (high - low) * rows
        return sum(dot(wt[n, at, lanes], ud[n, low:high].reshape(span, half)) for n in range(2))

    waiting = [0] + early
    low, high = spans[0]
    while any(low <= k < high for k in waiting):
        y_back[waiting.pop(0)].wait_recv()
    acc[...] = placed(slice(None), low, high)
    for k in waiting:
        y_back[k].wait_recv()
    c_back, writes = {}, []
    for n in range(2):
        at = slice(n * seg_local // 2, (n + 1) * seg_local // 2)
        done[at] = (acc[at] + placed(at, *spans[1]) + placed(at, *spans[2])).astype(BF16)
        c_back[n] = send(C_BACK, n, done.at[at], other_hbm.at[at], c_rep, me)
        c_back[n].start()
        writes.append(pltpu.make_async_copy(done.at[at], own_hbm.at[at], local_sem.at[n]))
        writes[n].start()
    for n in c_back:
        c_back[n].wait_recv()
    pair.wait_send()
    for group in (y_out, z_out, c_out, z_back, y_back, c_back):
        for k in group:
            group[k].wait_send()
    for write in writes:
        write.wait()


def join(own_hbm, other_hbm, out_hbm, whole, in_sem, out_sem):
    c = lax.rem(lax.axis_index("rep"), 2)
    seg_local, half = own_hbm.shape
    step = seg_local // JOINS
    reads, writes = [], []
    for i in range(JOINS):
        at = pl.ds(i * step, step)
        for n, (ref, side) in enumerate(((own_hbm, c), (other_hbm, 1 - c))):
            lanes = pl.ds(pl.multiple_of(side * half, half), half)
            reads.append(pltpu.make_async_copy(ref.at[at], whole.at[at, lanes], in_sem.at[n, i]))
            reads[-1].start()
    for i in range(JOINS):
        at = pl.ds(i * step, step)
        reads[2 * i].wait()
        reads[2 * i + 1].wait()
        writes.append(pltpu.make_async_copy(whole.at[at], out_hbm.at[at], out_sem.at[i]))
        writes[-1].start()
    for write in writes:
        write.wait()


def on_device(grad_part, seg_slot, owner, left_code, left_scale, right_code, right_scale):
    shards, reps = lax.axis_size("shard"), lax.axis_size("rep")
    assert reps % 4 == 0 and left_code.shape[0] == 2
    if reps > 4:
        every = lax.all_gather(grad_part[0], "rep").astype(F32)
        sums = jnp.sum(every.reshape((reps // 4, 4) + every.shape[1:]), axis=0)
        grad_part = sums[lax.axis_index("rep") % 4][None].astype(BF16)
    _, seg_local, width = grad_part.shape
    half = width // 2
    blocks, order_b = seg_slot.shape
    rows = order_b // shards
    flat = shards * rows
    hbm = pl.BlockSpec(memory_space=pltpu.HBM)
    own, other = pl.pallas_call(
        functools.partial(kernel, shards),
        out_shape=[jax.ShapeDtypeStruct((seg_local, half), BF16)] * 2,
        in_specs=[hbm] * 7,
        out_specs=[hbm, hbm],
        scratch_shapes=[
            pltpu.VMEM((blocks, order_b), jnp.int32),
            pltpu.VMEM((1, blocks), jnp.int32),
            pltpu.VMEM((2, order_b), F32),
            pltpu.VMEM((2, width), F32),
            pltpu.VMEM((seg_local, half), BF16),
            pltpu.VMEM((seg_local, half), BF16),
            pltpu.VMEM((2, seg_local, flat), BF16),
            pltpu.VMEM((2, shards, rows, half), BF16),
            pltpu.VMEM((shards, rows, half), BF16),
            pltpu.VMEM((shards, rows, half), BF16),
            pltpu.VMEM((2, shards, rows, half), BF16),
            pltpu.VMEM((order_b, order_b), BF16),
            pltpu.VMEM((2, half, width), BF16),
            pltpu.VMEM((flat, flat), BF16),
            pltpu.VMEM((flat, width), BF16),
            pltpu.VMEM((flat, width), F32),
            pltpu.VMEM((shards, rows, half), BF16),
            pltpu.VMEM((2, shards, rows, half), BF16),
            pltpu.VMEM((seg_local, half), F32),
            pltpu.VMEM((seg_local, half), BF16),
            pltpu.SemaphoreType.DMA((10,)),
            pltpu.SemaphoreType.DMA((7, shards)),
            pltpu.SemaphoreType.DMA((7, shards)),
        ],
        compiler_params=pltpu.CompilerParams(
            collective_id=0, has_side_effects=True, vmem_limit_bytes=60 * 1024 * 1024
        ),
    )(seg_slot, owner[None, :], left_scale, right_scale, grad_part, left_code, right_code)
    return pl.pallas_call(
        join,
        out_shape=jax.ShapeDtypeStruct((seg_local, width), BF16),
        in_specs=[hbm, hbm],
        out_specs=hbm,
        scratch_shapes=[
            pltpu.VMEM((seg_local, width), BF16),
            pltpu.SemaphoreType.DMA((2, JOINS)),
            pltpu.SemaphoreType.DMA((JOINS,)),
        ],
        compiler_params=pltpu.CompilerParams(vmem_limit_bytes=60 * 1024 * 1024),
    )(own, other)


def solution(mesh):
    in_specs = (
        P("rep", "shard", None),
        P(),
        P(),
        P("shard", None, None),
        P("shard", None),
        P("shard", None, None),
        P("shard", None),
    )
    out_specs = P("shard", None)
    return jax.shard_map(
        on_device, mesh=mesh, in_specs=in_specs, out_specs=out_specs, check_vma=False
    )
```

```python
import functools

import jax
import jax.numpy as jnp
from jax import lax
from jax.experimental import pallas as pl
from jax.experimental.pallas import tpu as pltpu
from jax.sharding import PartitionSpec as P

EPSILON = 1e-06
MESH = pl.DeviceIdType.MESH
F32 = jnp.float32
BF16 = jnp.bfloat16
Y_OUT, Z_OUT, C_OUT, Z_BACK, Y_BACK, C_BACK, PAIR = range(7)
JOINS = 2


def log2(value):
    assert value & (value - 1) == 0
    return value.bit_length() - 1


def iota(shape, dim):
    return lax.broadcasted_iota(jnp.int32, shape, dim)


def one_hot(mask):
    return jnp.where(mask, 1.0, 0.0).astype(BF16)


def dot(a, b, contract=((1,), (0,))):
    return lax.dot_general(a, b, (contract, ((), ())), preferred_element_type=F32)


def partner(me, k, shards):
    out = 0
    for j in range(log2(shards)):
        bit = lax.rem(lax.div(me, 1 << j), 2)
        out = out + (1 - bit if (k >> j) & 1 else bit) * (1 << j)
    return out


def send_order(shards):
    far = list(range(shards // 2, shards))
    near = [*range(shards // 4, shards // 2), *range(shards // 4 - 1, 0, -1)]
    order = far[:2]
    for n, k in enumerate(near):
        order += [k] + far[n + 2:n + 3]
    return order


def kernel(
    shards, seg_hbm, owner_hbm, lscale_hbm, rscale_hbm, grad_hbm, left_hbm, right_hbm,
    own_hbm, other_hbm,
    seg_ref, owner_ref, lscale_ref, rscale_ref, p_own, p_got, wt, f, y_got, g, a, left_v, right_v, lperm, mid, partial, u, ud, acc, done, local_sem, send_sem, recv_sem,
):
    rep, me = lax.axis_index("rep"), lax.axis_index("shard")
    y, c = lax.rem(lax.div(rep, 2), 2), lax.rem(rep, 2)
    y_rep, c_rep = rep + 2 - 4 * y, rep + 1 - 2 * c
    blocks, order_b = seg_ref.shape
    rows = order_b // shards
    seg_local, half = p_own.shape
    flat = shards * rows
    order = send_order(shards)
    peers = {k: partner(me, k, shards) for k in order}
    here = pl.ds(pl.multiple_of(c * half, half), half)
    there = pl.ds(pl.multiple_of((1 - c) * half, half), half)

    tables = [
        pltpu.make_async_copy(seg_hbm, seg_ref, local_sem.at[6]),
        pltpu.make_async_copy(owner_hbm, owner_ref, local_sem.at[7]),
    ]
    loads = [
        pltpu.make_async_copy(grad_hbm.at[0, :, here], p_own, local_sem.at[0]),
        pltpu.make_async_copy(left_hbm.at[y], left_v, local_sem.at[1]),
    ]
    for i, r in enumerate((here, there)):
        for j, w in enumerate((here, there)):
            loads.append(pltpu.make_async_copy(
                right_hbm.at[y, r, w], right_v.at[i, :, pl.ds(j * half, half)], local_sem.at[2 + 2 * i + j]))
    loads.append(pltpu.make_async_copy(lscale_hbm, lscale_ref, local_sem.at[8]))
    loads.append(pltpu.make_async_copy(rscale_hbm, rscale_ref, local_sem.at[9]))

    def send(kind, k, src, dst, rep_to, shard_to):
        return pltpu.make_async_remote_copy(
            src_ref=src, dst_ref=dst, send_sem=send_sem.at[kind, k], recv_sem=recv_sem.at[kind, k],
            device_id={"rep": rep_to, "shard": shard_to}, device_id_type=MESH)

    for load in tables + loads[:1]:
        load.start()
    barrier = pltpu.get_barrier_semaphore()
    pl.semaphore_signal(barrier, inc=1, device_id={"rep": c_rep, "shard": me}, device_id_type=MESH)
    pl.semaphore_signal(barrier, inc=1, device_id={"rep": y_rep, "shard": me}, device_id_type=MESH)
    for k in order:
        pl.semaphore_signal(barrier, inc=1, device_id={"rep": rep, "shard": peers[k]}, device_id_type=MESH)
    pl.semaphore_wait(barrier, 2 + len(order))

    pair = send(PAIR, 0, grad_hbm.at[0, :, there], p_got, c_rep, me)
    pair.start()
    for load in loads[1:]:
        load.start()
    gather = one_hot((iota((flat, order_b), 1) >> log2(shards)) == (iota((flat, order_b), 0) & (rows - 1)))

    for load in tables:
        load.wait()
    seg = seg_ref[...]
    local = seg - me * seg_local
    local = jnp.where((local >= 0) & (local < seg_local), local, 0)
    digits = jnp.concatenate([local >> 4, local & 15], axis=0).astype(F32).astype(BF16)
    found = dot(gather, digits, ((1,), (1,)))
    place_of = found[:, :blocks] * 16.0 + found[:, blocks:] + 1.0
    own_row = owner_ref[...].astype(F32)
    line_b, lane_b = iota((blocks, blocks), 0), iota((blocks, blocks), 1)
    own_col = jnp.sum(jnp.where(line_b == lane_b, own_row, 0.0), axis=1, keepdims=True)
    same = own_col == own_row
    key_row = own_row * 2.0 + jnp.sum(jnp.where(same & (line_b < lane_b), 1.0, 0.0), axis=0, keepdims=True)
    key = own_col * 2.0 + jnp.sum(jnp.where(same & (lane_b < line_b), 1.0, 0.0), axis=1, keepdims=True)
    peer_col = (iota((flat, 1), 0) >> log2(rows)) ^ me
    seg_lane = iota((flat, seg_local), 1).astype(F32)

    def picked(plane):
        wanted = (peer_col * 2 + lax.rem(y + plane, 2)).astype(F32)
        place = jnp.sum(jnp.where(key_row == wanted, place_of, 0.0), axis=1, keepdims=True) - 1.0
        return one_hot(seg_lane == place)

    pick_far = picked(1)
    loads[0].wait()
    pair.wait_recv()
    q = (p_own[...].astype(F32) + p_got[...].astype(F32)).astype(BF16)
    quarter = shards // 4
    spans = ((quarter, 3 * quarter), (0, quarter), (3 * quarter, shards))
    y_out = {k: send(Y_OUT, k, f.at[1, k], y_got.at[k], y_rep, me) for k in order + [0]}
    unsent = order + [0]
    for n, (low, high) in enumerate(spans):
        part = dot(pick_far[low * rows:high * rows], q)
        f[1, low:high] = part.astype(BF16).reshape(high - low, rows, half)
        while unsent and n == 0 and low <= unsent[0] < high:
            y_out[unsent.pop(0)].start()
    for k in unsent:
        y_out[k].start()
    f[0] = dot(picked(0), q).astype(BF16).reshape(shards, rows, half)
    z_out = {k: send(Z_OUT, k, g.at[k], a.at[0, k], rep, peers[k]) for k in order}
    c_out = {
        n: send(C_OUT, n, a.at[0, low:high], a.at[1, low:high], c_rep, me) for n, (low, high) in enumerate(spans)
    }

    def pass_on(k):
        y_out[k].wait_recv()
        total = (f[0, k].astype(F32) + y_got[k].astype(F32)).astype(BF16)
        if k:
            g[k] = total
            z_out[k].start()
        else:
            a[0, 0] = total

    for k in order[:-1]:
        pass_on(k)

    for load in loads[1:]:
        load.wait()
    mine = key == (me * 2 + y).astype(F32)
    first = (seg[:, 0:1] >> log2(seg_local)).astype(F32)
    shift = jnp.sum(jnp.where(mine, first, 0.0), axis=0, keepdims=True).astype(jnp.int32)
    line = iota((flat, 1), 0)
    target = (line & (rows - 1)) * shards + ((((line >> log2(rows)) ^ me) - shift) & (shards - 1))
    chosen = iota((flat, order_b), 1) == target
    lscale = jnp.where(y == 0, lscale_ref[0:1, :], lscale_ref[1:2, :])
    lscale = jnp.sum(jnp.where(chosen, lscale, 0.0), axis=1, keepdims=True)
    rscale = jnp.where(y == 0, rscale_ref[0:1, :], rscale_ref[1:2, :])
    rscale = jnp.where(c == 0, rscale, jnp.concatenate([rscale[:, half:], rscale[:, :half]], axis=1))
    turn = one_hot(chosen)
    lperm[...] = dot(dot(turn, left_v[...]).astype(BF16), turn, ((1,), (1,))).astype(BF16)

    for k in order[-1:] + [0]:
        pass_on(k)
    late = order[:-2] + [order[-1], order[-2]]
    early = [order[2], order[0]] + sorted(set(range(1, shards // 2)) - {order[2]}, reverse=True) + order[1:2]
    early += sorted(set(range(shards // 2, shards)) - set(order[:2]))
    waiting = list(late)

    def middle(n):
        low, high = spans[n]
        c_out[n].wait_recv()
        span = (high - low) * rows
        mine_half = a[0, low:high].reshape(span, half)
        other_half = a[1, low:high].reshape(span, half)
        part = dot(mine_half, right_v[0]) + dot(other_half, right_v[1])
        mid[low * rows:high * rows] = (part * rscale).astype(BF16)
        wide, wide_other = mine_half.astype(F32), other_half.astype(F32)
        return jnp.sum(wide * wide + wide_other * wide_other, keepdims=True)

    grad_power = jnp.zeros((1, 1), F32)
    for n, (low, high) in enumerate(spans):
        while any(low <= k < high for k in waiting):
            z_out[waiting.pop(0)].wait_recv()
        c_out[n].start()
        if n:
            grad_power += middle(n - 1)
    known = 3 * quarter * rows
    partial[...] = dot(lperm[:, :known], mid[:known])
    grad_power += middle(len(spans) - 1)

    precond = (partial[...] + dot(lperm[:, known:], mid[known:])) * lscale
    update_power = jnp.sum(precond * precond, keepdims=True)
    scale = 1.0 / (order_b * 2 * half)
    ratio = jnp.sqrt((grad_power * scale + EPSILON) / (update_power * scale + EPSILON))
    u[...] = (precond[:, :half] * ratio).astype(BF16).reshape(shards, rows, half)

    z_back = {k: send(Z_BACK, k, u.at[k], ud.at[0, k], rep, peers[k]) for k in order}
    y_back = {k: send(Y_BACK, k, ud.at[0, k], ud.at[1, k], y_rep, me) for k in order + [0]}
    for k in order:
        z_back[k].start()
    ud[0, 0] = u[0]
    y_back[0].start()
    mid_way = shards // 2
    for k in early[:mid_way]:
        z_back[k].wait_recv()
        y_back[k].start()

    spread = one_hot((iota((order_b, flat), 0) >> log2(shards)) == (iota((order_b, flat), 1) & (rows - 1)))
    found = dot(digits, spread)
    place_of = found[:blocks] * 16.0 + found[blocks:] + 1.0
    peer_row = (iota((1, flat), 1) >> log2(rows)) ^ me
    seg_id = iota((seg_local, flat), 0).astype(F32)
    for plane in range(2):
        wanted = (peer_row * 2 + lax.rem(y + plane, 2)).astype(F32)
        place = jnp.sum(jnp.where(key == wanted, place_of, 0.0), axis=0, keepdims=True) - 1.0
        wt[plane] = one_hot(seg_id == place)
    for k in early[mid_way:]:
        z_back[k].wait_recv()
        y_back[k].start()

    def placed(at, low, high):
        lanes = slice(low * rows, high * rows)
        span = (high - low) * rows
        return sum(dot(wt[n, at, lanes], ud[n, low:high].reshape(span, half)) for n in range(2))

    waiting = [0] + early
    low, high = spans[0]
    while any(low <= k < high for k in waiting):
        y_back[waiting.pop(0)].wait_recv()
    acc[...] = placed(slice(None), low, high)
    for k in waiting:
        y_back[k].wait_recv()
    c_back, writes = {}, []
    for n in range(2):
        at = slice(n * seg_local // 2, (n + 1) * seg_local // 2)
        done[at] = (acc[at] + placed(at, *spans[1]) + placed(at, *spans[2])).astype(BF16)
        c_back[n] = send(C_BACK, n, done.at[at], other_hbm.at[at], c_rep, me)
        c_back[n].start()
        writes.append(pltpu.make_async_copy(done.at[at], own_hbm.at[at], local_sem.at[n]))
        writes[n].start()
    for n in c_back:
        c_back[n].wait_recv()
    pair.wait_send()
    for group in (y_out, z_out, c_out, z_back, y_back, c_back):
        for k in group:
            group[k].wait_send()
    for write in writes:
        write.wait()


def join(own_hbm, other_hbm, out_hbm, whole, in_sem, out_sem):
    c = lax.rem(lax.axis_index("rep"), 2)
    seg_local, half = own_hbm.shape
    step = seg_local // JOINS
    reads, writes = [], []
    for i in range(JOINS):
        at = pl.ds(i * step, step)
        for n, (ref, side) in enumerate(((own_hbm, c), (other_hbm, 1 - c))):
            lanes = pl.ds(pl.multiple_of(side * half, half), half)
            reads.append(pltpu.make_async_copy(ref.at[at], whole.at[at, lanes], in_sem.at[n, i]))
            reads[-1].start()
    for i in range(JOINS):
        at = pl.ds(i * step, step)
        reads[2 * i].wait()
        reads[2 * i + 1].wait()
        writes.append(pltpu.make_async_copy(whole.at[at], out_hbm.at[at], out_sem.at[i]))
        writes[-1].start()
    for write in writes:
        write.wait()


def on_device(grad_part, seg_slot, owner, left_code, left_scale, right_code, right_scale):
    shards, reps = lax.axis_size("shard"), lax.axis_size("rep")
    assert reps % 4 == 0 and left_code.shape[0] == 2
    if reps > 4:
        every = lax.all_gather(grad_part[0], "rep").astype(F32)
        sums = jnp.sum(every.reshape((reps // 4, 4) + every.shape[1:]), axis=0)
        grad_part = sums[lax.axis_index("rep") % 4][None].astype(BF16)
    _, seg_local, width = grad_part.shape
    half = width // 2
    blocks, order_b = seg_slot.shape
    rows = order_b // shards
    flat = shards * rows
    hbm = pl.BlockSpec(memory_space=pltpu.HBM)
    own, other = pl.pallas_call(
        functools.partial(kernel, shards),
        out_shape=[jax.ShapeDtypeStruct((seg_local, half), BF16)] * 2,
        in_specs=[hbm] * 7,
        out_specs=[hbm, hbm],
        scratch_shapes=[
            pltpu.VMEM((blocks, order_b), jnp.int32),
            pltpu.VMEM((1, blocks), jnp.int32),
            pltpu.VMEM((2, order_b), F32),
            pltpu.VMEM((2, width), F32),
            pltpu.VMEM((seg_local, half), BF16),
            pltpu.VMEM((seg_local, half), BF16),
            pltpu.VMEM((2, seg_local, flat), BF16),
            pltpu.VMEM((2, shards, rows, half), BF16),
            pltpu.VMEM((shards, rows, half), BF16),
            pltpu.VMEM((shards, rows, half), BF16),
            pltpu.VMEM((2, shards, rows, half), BF16),
            pltpu.VMEM((order_b, order_b), BF16),
            pltpu.VMEM((2, half, width), BF16),
            pltpu.VMEM((flat, flat), BF16),
            pltpu.VMEM((flat, width), BF16),
            pltpu.VMEM((flat, width), F32),
            pltpu.VMEM((shards, rows, half), BF16),
            pltpu.VMEM((2, shards, rows, half), BF16),
            pltpu.VMEM((seg_local, half), F32),
            pltpu.VMEM((seg_local, half), BF16),
            pltpu.SemaphoreType.DMA((10,)),
            pltpu.SemaphoreType.DMA((7, shards)),
            pltpu.SemaphoreType.DMA((7, shards)),
        ],
        compiler_params=pltpu.CompilerParams(
            collective_id=0, has_side_effects=True, vmem_limit_bytes=60 * 1024 * 1024
        ),
    )(seg_slot, owner[None, :], left_scale, right_scale, grad_part, left_code, right_code)
    return pl.pallas_call(
        join,
        out_shape=jax.ShapeDtypeStruct((seg_local, width), BF16),
        in_specs=[hbm, hbm],
        out_specs=hbm,
        scratch_shapes=[
            pltpu.VMEM((seg_local, width), BF16),
            pltpu.SemaphoreType.DMA((2, JOINS)),
            pltpu.SemaphoreType.DMA((JOINS,)),
        ],
        compiler_params=pltpu.CompilerParams(vmem_limit_bytes=60 * 1024 * 1024),
    )(own, other)


def solution(mesh):
    in_specs = (
        P("rep", "shard", None),
        P(),
        P(),
        P("shard", None, None),
        P("shard", None),
        P("shard", None, None),
        P("shard", None),
    )
    out_specs = P("shard", None)
    return jax.shard_map(
        on_device, mesh=mesh, in_specs=in_specs, out_specs=out_specs, check_vma=False
    )
```
